256 devices in a mesh: store: 64 (over x, z_lo, y, core), tensor: 4 (over z_hi).
Axes of the slice: x: 4, y: 4, z: 8 (z_hi: 4, z_lo: 2; z = z_hi * 2 + z_lo), core: 2. Of those that a mesh axis runs over, the one named last changes fastest.
Arguments:
- test_inputs: bfloat16 [128, 512, 5120], P('store', None, 'tensor'), may hold values from -6 to 6
- test_cotangents: bfloat16 [128, 512, 5120], P('store', 'tensor'), may hold values from -6 to 6
- train_inputs: bfloat16 [64, 512, 5120], P('store', None, 'tensor'), may hold values from -6 to 6
- train_cotangents: bfloat16 [64, 512, 5120], P('store', 'tensor'), may hold values from -6 to 6
- test_lengths: int32 [128], P('store'), may hold values from 64 to 512, as said below
- train_lengths: int32 [64], P('store'), may hold values from 64 to 512, as said below
- in_projection: bfloat16 [64, 5120], P(None, 'tensor'), may hold values from -0.078125 to 0.078125
- out_projection: bfloat16 [64, 5120], replicated, may hold values from -0.078125 to 0.078125
- in_inverse: float32 [64, 64], replicated, as said below
- out_inverse: float32 [64, 64], replicated, as said below
- store: bfloat16 [131072, 4096], P(('store', 'tensor')), may hold values from -0.59765625 to 0.59765625
Outputs:
- store_scores: float32 [128, 131072], P(None, ('store', 'tensor'))
- fresh_scores: float32 [128, 64], P(None, 'store')
The draws below stay inside these ranges and needn't reach their ends.
Inputs may be any that keep to these rules, and one draw needn't show every extreme that they name: `test_lengths`: positions at or past a pair's length are padding. `train_lengths`: positions at or past a pair's length are padding. `in_inverse`: symmetric positive definite. `out_inverse`: symmetric positive definite.
All inputs are finite; a program needn't handle non-finite values.
Results may differ from the reference program's by a relative error of at most 0.024.
Values may be sent and summed in bfloat16 or wider, within the bound.
A program may use at most 128 MiB of HBM per device.

```python
import jax
import jax.numpy as jnp
from jax import lax

D = 5120
R = 64
LEN = 512
TESTS = 128
TRAINS = 64
STORE = 131072


def draw_lengths(key, count):
    values = jax.random.randint(key, (count,), -(LEN // 2), 2 * LEN)
    return jnp.clip(values, LEN // 8, LEN).astype(jnp.int32)


def draw_test_lengths(key, part):
    key = jax.random.fold_in(key, 11)
    return draw_lengths(key, TESTS)


def draw_train_lengths(key, part):
    key = jax.random.fold_in(key, 12)
    return draw_lengths(key, TRAINS)


def draw_inverse(key, offdiag_scale, low, high):
    first_key, second_key = jax.random.split(key)
    noise = jax.random.normal(first_key, (R, R), jnp.float32) * offdiag_scale
    symmetric = (noise + noise.T) * 0.7071
    diagonal = jax.random.uniform(second_key, (R,), jnp.float32, low, high)
    identity = (jnp.arange(R)[:, None] == jnp.arange(R)[None, :]).astype(jnp.float32)
    return symmetric * (1.0 - identity) + identity * diagonal[None, :]


def draw_in_inverse(key, part):
    key = jax.random.fold_in(key, 13)
    return draw_inverse(key, 0.04, 1.0, 4.0)


def draw_out_inverse(key, part):
    key = jax.random.fold_in(key, 14)
    return draw_inverse(key, 0.04, 1.0, 4.0)


def level_of(stream_key, extent, cuts, low, high):
    level = 1.0
    for dim, blocks in cuts:
        steps = jax.random.uniform(jax.random.fold_in(jax.random.fold_in(stream_key, 6), dim), (blocks,), jnp.float32, low / len(cuts), high / len(cuts))
        level = level * jnp.repeat(jnp.exp(steps), extent[dim] // blocks).reshape((-1,) + (1,) * (len(extent) - 1 - dim))
    return level


def bell_draw(key, dims, scale, limit, cuts=(), held_as=jnp.bfloat16):
    loudness = level_of(key, dims, cuts, -0.22, 0.18) if cuts else 1.0
    entries = jax.random.normal(key, dims, jnp.float32) * scale * loudness
    return jnp.minimum(jnp.maximum(entries, -limit), limit).astype(held_as)


def setup_inputs(seed: int = 0) -> dict:
    arg_keys = jax.random.split(jax.random.key(seed), 12)
    test_inputs = bell_draw(arg_keys[0], (TESTS, LEN, D), 1.0, 6.0, ((0, 64), (2, 4)))
    test_cotangents = bell_draw(arg_keys[1], (TESTS, LEN, D), 1.0, 6.0, ((0, 64), (1, 4)))
    train_inputs = bell_draw(arg_keys[2], (TRAINS, LEN, D), 1.0, 6.0, ((0, 64), (2, 4)))
    train_cotangents = bell_draw(arg_keys[3], (TRAINS, LEN, D), 1.0, 6.0, ((0, 64), (1, 4)))
    test_lengths = draw_test_lengths(jax.random.fold_in(arg_keys[11], 71), 0)
    train_lengths = draw_train_lengths(jax.random.fold_in(arg_keys[11], 71), 0)
    in_projection = bell_draw(arg_keys[6], (R, D), D ** -0.5, 0.078125, ((1, 4),))
    out_projection = bell_draw(arg_keys[7], (R, D), D ** -0.5, 0.078125)
    in_inverse = draw_in_inverse(jax.random.fold_in(arg_keys[11], 71), 0)
    out_inverse = draw_out_inverse(jax.random.fold_in(arg_keys[11], 71), 0)
    store = bell_draw(arg_keys[10], (STORE, R * R), 0.1, 0.59765625, ((0, 256),))
    return dict(test_inputs=test_inputs, test_cotangents=test_cotangents, train_inputs=train_inputs, train_cotangents=train_cotangents, test_lengths=test_lengths, train_lengths=train_lengths, in_projection=in_projection, out_projection=out_projection, in_inverse=in_inverse, out_inverse=out_inverse, store=store)


def pair_factors(inputs, cotangents, lengths, in_projection, out_projection):
    in_weights = in_projection.astype(jnp.float32)
    out_weights = out_projection.astype(jnp.float32)
    positions = jnp.arange(LEN, dtype=jnp.int32)

    def single(items):
        one_in, one_out, length = items
        projected_in = jnp.einsum("ld,rd->rl", one_in.astype(jnp.float32), in_weights)
        projected_out = jnp.einsum("ld,rd->rl", one_out.astype(jnp.float32), out_weights)
        kept_mask = (positions < length).astype(jnp.float32)
        projected_out = projected_out * kept_mask[None, :] / length.astype(jnp.float32)
        return jnp.einsum("ol,il->oi", projected_out, projected_in)

    return lax.map(single, (inputs, cotangents, lengths))


def reference(test_inputs, test_cotangents, train_inputs, train_cotangents, test_lengths, train_lengths, in_projection, out_projection, in_inverse, out_inverse, store):
    test_factors = pair_factors(test_inputs, test_cotangents, test_lengths, in_projection, out_projection)
    train_factors = pair_factors(train_inputs, train_cotangents, train_lengths, in_projection, out_projection)
    highest = lax.Precision.HIGHEST
    conditioned = jnp.einsum("ab,nbc->nac", out_inverse, test_factors, precision=highest)
    conditioned = jnp.einsum("nac,cd->nad", conditioned, in_inverse, precision=highest)
    conditioned = conditioned.astype(jnp.bfloat16).reshape(conditioned.shape[0], R * R)
    train_flat = train_factors.astype(jnp.bfloat16).reshape(train_factors.shape[0], R * R)
    store_scores = lax.dot_general(conditioned, store, (((1,), (1,)), ((), ())), preferred_element_type=jnp.float32)
    fresh_scores = lax.dot_general(conditioned, train_flat, (((1,), (1,)), ((), ())), preferred_element_type=jnp.float32)
    return store_scores, fresh_scores
```

```python
import jax
import jax.numpy as jnp
from jax import lax
from jax.experimental import pallas as pl
from jax.experimental.pallas import tpu as pltpu
from jax.sharding import PartitionSpec as P

MESH = pl.DeviceIdType.MESH
F32 = jnp.float32
BF16 = jnp.bfloat16
HIGHEST = lax.Precision.HIGHEST
NT = (((1,), (1,)), ((), ()))

NX, NZL, NY, NC, NT4 = 4, 2, 4, 2, 4
R = 64
QUARTER = 128
LEN = 512
HALF = 2048
CHUNKS = 2
CHUNK = HALF // CHUNKS


def remote(src, dst, send_sem, recv_sem, device):
    return pltpu.make_async_remote_copy(
        src_ref=src,
        dst_ref=dst,
        send_sem=send_sem,
        recv_sem=recv_sem,
        device_id=device,
        device_id_type=MESH,
    )


def mod4(value):
    return lax.rem(value + 4, 4)


def kernel(
    tin_ref,
    tcot_ref,
    rin_ref,
    rcot_ref,
    tlen_ref,
    rlen_ref,
    win_ref,
    wout_ref,
    iinv_ref,
    oinv_ref,
    store_ref,
    scores_ref,
    fresh_ref,
    tin,
    tcot,
    rin,
    rcot,
    win,
    wout,
    iinv,
    oinv,
    store,
    po,
    part_send,
    part_recv,
    mine,
    gath,
    swap,
    full,
    acc,
    accf,
    rpo,
    rscr,
    rpart_send,
    rpart_recv,
    trow,
    trowb,
    load_sem,
    po_send,
    po_recv,
    rs_send,
    rs_recv,
    col_send,
    col_recv,
    s4_send,
    s4_recv,
    s5_send,
    s5_recv,
    fw_send,
    fw_recv,
    rpo_send,
    rpo_recv,
    rrs_send,
    rrs_recv,
):
    me = lax.axis_index("store")
    t = lax.axis_index("tensor")
    c = lax.rem(me, 2)
    y = lax.rem(lax.div(me, 2), 4)
    zl = lax.rem(lax.div(me, 8), 2)
    x = lax.div(me, 16)

    def index(xx, zz, yy, cc):
        return ((xx * 2 + zz) * 4 + yy) * 2 + cc

    early = [
        pltpu.make_async_copy(wout_ref, wout, load_sem.at[0]),
        pltpu.make_async_copy(tcot_ref, tcot, load_sem.at[1]),
        pltpu.make_async_copy(oinv_ref, oinv, load_sem.at[2]),
        pltpu.make_async_copy(iinv_ref, iinv, load_sem.at[3]),
        pltpu.make_async_copy(win_ref, win, load_sem.at[4]),
        pltpu.make_async_copy(tin_ref, tin, load_sem.at[5]),
    ]
    late = [
        pltpu.make_async_copy(rcot_ref.at[0], rcot, load_sem.at[6]),
        pltpu.make_async_copy(rin_ref.at[0], rin, load_sem.at[7]),
        pltpu.make_async_copy(store_ref, store, load_sem.at[8]),
    ]
    for copy in early:
        copy.start()

    barrier = pltpu.get_barrier_semaphore()
    partners = []
    for dt in range(4):
        for dz in range(2):
            for dc in range(2):
                if dt or dz or dc:
                    partners.append(
                        (index(x, lax.rem(zl + dz, 2), y, lax.rem(c + dc, 2)), mod4(t + dt))
                    )
    for k in range(1, 4):
        partners.append((index(mod4(x + k), zl, y, c), t))
        partners.append((index(x, zl, mod4(y + k), c), t))
    for partner in partners:
        pl.semaphore_signal(barrier, inc=1, device_id=partner, device_id_type=MESH)

    lane = lax.broadcasted_iota(jnp.int32, (1, QUARTER), 1) + t * QUARTER

    def scale_of(length):
        lengths = jnp.full((1, QUARTER), length, jnp.int32)
        kept = jnp.where(lane < lengths, 1.0, 0.0).astype(F32)
        return kept / lengths.astype(F32)

    early[0].wait()
    early[1].wait()
    pout = lax.dot_general(
        wout[...], tcot[...].reshape(2 * QUARTER, 5120), NT, preferred_element_type=F32
    )
    scale = jnp.concatenate([scale_of(tlen_ref[0]), scale_of(tlen_ref[1])], axis=1)
    pout = pout * scale
    early[2].wait()
    left = jnp.concatenate(
        [oinv[pl.ds(0, 32, stride=2), :], oinv[pl.ds(1, 32, stride=2), :]], axis=0
    )
    pout = jnp.dot(left, pout, precision=HIGHEST, preferred_element_type=F32)
    po[t] = pout.astype(BF16)

    pl.semaphore_wait(barrier, len(partners))
    po_copies = []
    for k in range(1, 4):
        copy = remote(
            po.at[t], po.at[t], po_send.at[k - 1], po_recv.at[k - 1], (me, mod4(t + k))
        )
        copy.start()
        po_copies.append(copy)
    for copy in late:
        copy.start()

    early[3].wait()
    early[4].wait()
    early[5].wait()
    pin = lax.dot_general(
        win[...], tin[...].reshape(2 * LEN, 1280), NT, preferred_element_type=F32
    )
    pin = jnp.dot(iinv[...], pin, precision=HIGHEST, preferred_element_type=F32)
    pin = pin.astype(BF16)

    late[0].wait()
    rout = lax.dot_general(wout[...], rcot[...], NT, preferred_element_type=F32)
    rout = rout * scale_of(rlen_ref[0])
    rpo[t] = rout.astype(BF16)
    late[1].wait()
    rpin = lax.dot_general(win[...], rin[...], NT, preferred_element_type=F32).astype(BF16)

    for k in range(1, 4):
        slot = mod4(t - k)
        remote(
            po.at[slot], po.at[slot], po_send.at[k - 1], po_recv.at[k - 1], (me, slot)
        ).wait_recv()

    for n in range(2):
        outs = jnp.concatenate(
            [po[u, :, n * QUARTER : (n + 1) * QUARTER] for u in range(4)], axis=1
        )
        part = lax.dot_general(
            outs, pin[:, n * LEN : (n + 1) * LEN], NT, preferred_element_type=F32
        )
        packed = jnp.concatenate([part[:32], part[32:]], axis=1)
        for u in range(4):
            part_send[u, n] = packed[8 * u : 8 * u + 8]

    rs_copies = []
    for k in range(1, 4):
        to = mod4(t + k)
        copy = remote(
            part_send.at[to], part_recv.at[k - 1], rs_send.at[k - 1], rs_recv.at[k - 1], (me, to)
        )
        copy.start()
        rs_copies.append(copy)
    for copy in rs_copies:
        copy.wait_recv()
    total = part_send[t] + part_recv[0] + part_recv[1] + part_recv[2]
    mine[...] = total.reshape(16, 128).astype(BF16)

    h = lax.div(t, 2)
    a_h = x * (1 - h) + y * h
    slot = (zl * 2 + c) * 2 + lax.rem(t, 2)
    col_copies = []
    for dt in range(4):
        for dz in range(2):
            i = dt * 2 + dz
            if i:
                copy = remote(
                    mine,
                    gath.at[a_h, slot],
                    col_send.at[i],
                    col_recv.at[slot],
                    (index(x, lax.rem(zl + dz, 2), y, h), mod4(t + dt)),
                )
                copy.start()
                col_copies.append(copy)

    own_copy = pltpu.make_async_copy(mine, gath.at[a_h, slot], col_recv.at[slot])
    sib_copy = remote(
        mine, gath.at[a_h, slot], col_send.at[0], col_recv.at[slot], (index(x, zl, y, h), t)
    )

    @pl.when(h == c)
    def _():
        own_copy.start()

    @pl.when(h != c)
    def _():
        sib_copy.start()

    rpo_copies = []
    for k in range(1, 4):
        copy = remote(
            rpo.at[t], rpo.at[t], rpo_send.at[k - 1], rpo_recv.at[k - 1], (me, mod4(t + k))
        )
        copy.start()
        rpo_copies.append(copy)

    a = x * (1 - c) + y * c
    for i in range(8):
        pltpu.make_async_copy(mine, gath.at[a, i], col_recv.at[i]).wait()

    s4_copies = []
    for k in range(1, 4):
        to = index(mod4(x + k * (1 - c)), zl, mod4(y + k * c), c)
        copy = remote(gath.at[a], gath.at[a], s4_send.at[k - 1], s4_recv.at[k - 1], (to, t))
        copy.start()
        s4_copies.append(copy)

    for k in range(1, 4):
        from_t = mod4(t - k)
        remote(
            rpo.at[from_t], rpo.at[from_t], rpo_send.at[k - 1], rpo_recv.at[k - 1], (me, from_t)
        ).wait_recv()
    routs = jnp.concatenate([rpo[u] for u in range(4)], axis=1)
    rscr[...] = lax.dot_general(routs, rpin, NT, preferred_element_type=F32)
    rpart_send[...] = jnp.concatenate(
        [rscr[pl.ds(0, 32, stride=2), :], rscr[pl.ds(1, 32, stride=2), :]], axis=1
    )
    rrs_copies = []
    for k in range(1, 4):
        copy = remote(
            rpart_send,
            rpart_recv.at[k - 1],
            rrs_send.at[k - 1],
            rrs_recv.at[k - 1],
            (me, mod4(t + k)),
        )
        copy.start()
        rrs_copies.append(copy)

    for k in range(1, 4):
        slot_in = mod4(a - k)
        remote(
            gath.at[slot_in], gath.at[slot_in], s4_send.at[k - 1], s4_recv.at[k - 1], (me, t)
        ).wait_recv()

    q = y * (1 - c) + x * c
    for pair in range(2):
        for j in range(2):
            blocks = []
            for aa in (2 * pair, 2 * pair + 1):
                rows = [gath[aa, s * 2 + j].astype(F32).reshape(2, 8, 128) for s in range(4)]
                blocks.append(jnp.swapaxes(jnp.concatenate(rows, axis=0), 0, 1))
            both = jnp.concatenate(blocks, axis=1).astype(BF16)
            for e in range(8):
                full[c, j, q, pair * 16 : pair * 16 + 16, e * 128 : (e + 1) * 128] = both[e]

    sib = index(x, zl, y, 1 - c)
    s5_copies, fw_copies = [], []

    def forward(j, i, at):
        copy = remote(
            full.at[c, j, at], full.at[c, j, at], fw_send.at[j, i], fw_recv.at[j, i], (sib, t)
        )
        copy.start()
        fw_copies.append(copy)

    for j in range(CHUNKS):
        for k in range(1, 4):
            to = index(mod4(x + k * c), zl, mod4(y + k * (1 - c)), c)
            copy = remote(
                full.at[c, j, q],
                full.at[c, j, q],
                s5_send.at[j, k - 1],
                s5_recv.at[j, k - 1],
                (to, t),
            )
            copy.start()
            s5_copies.append(copy)
    for j in range(CHUNKS):
        forward(j, 0, q)

    for copy in rrs_copies:
        copy.wait_recv()
    rtotal = rpart_send[...] + rpart_recv[0] + rpart_recv[1] + rpart_recv[2]
    trow[...] = jnp.zeros_like(trow)
    for e in range(32):
        trow[0:1, e * 128 : (e + 1) * 128] = rtotal[e : e + 1]
    trowb[...] = trow[...].astype(BF16)

    late[2].wait()

    def scores_of(hh, j):
        lhs = full[hh, j].reshape(4 * 32, CHUNK)
        columns = pl.ds(pl.multiple_of(hh * HALF + j * CHUNK, 128), CHUNK)
        value = lax.dot_general(lhs, store[:, columns], NT, preferred_element_type=F32)
        valuef = lax.dot_general(lhs, trowb[:, columns], NT, preferred_element_type=F32)
        if j == 0:
            acc[hh] = value
            accf[hh] = valuef
        else:
            acc[hh] += value
            accf[hh] += valuef

    for j in range(CHUNKS):
        for k in range(1, 4):
            at = mod4(q - k)
            remote(
                full.at[c, j, at], full.at[c, j, at], s5_send.at[j, k - 1], s5_recv.at[j, k - 1], (me, t)
            ).wait_recv()
            forward(j, k, at)
        scores_of(c, j)
    for j in range(CHUNKS):
        for i in range(4):
            at = mod4(a - i)
            remote(
                full.at[1 - c, j, at], full.at[1 - c, j, at], fw_send.at[j, i], fw_recv.at[j, i], (sib, t)
            ).wait_recv()
        scores_of(1 - c, j)

    for xx in range(4):
        for yp in range(2):
            block, blockf = [], []
            for yy in (2 * yp, 2 * yp + 1):
                i0, i1 = (yy * 4 + xx) * 8, (xx * 4 + yy) * 8
                block.append(acc[0, i0 : i0 + 8] + acc[1, i1 : i1 + 8])
                blockf.append(accf[0, i0 : i0 + 8] + accf[1, i1 : i1 + 8])
            for zz in range(2):
                row = xx * 32 + zz * 16 + yp * 8
                cut = slice(zz * 4, zz * 4 + 4)
                scores_ref[row : row + 8, :] = jnp.concatenate([b[cut] for b in block], axis=0)
                fresh_ref[row : row + 8, :] = jnp.concatenate(
                    [b[cut, 0:1] for b in blockf], axis=0
                )

    for copy in (
        po_copies + rs_copies + col_copies + rpo_copies + s4_copies + rrs_copies + s5_copies + fw_copies
    ):
        copy.wait_send()

    @pl.when(h != c)
    def _():
        sib_copy.wait_send()


def body(*args):
    dma = pltpu.SemaphoreType.DMA
    anywhere = pl.BlockSpec(memory_space=pl.ANY)
    smem = pl.BlockSpec(memory_space=pltpu.SMEM)
    vmem = pl.BlockSpec(memory_space=pltpu.VMEM)
    return pl.pallas_call(
        kernel,
        out_shape=(
            jax.ShapeDtypeStruct((128, 512), F32),
            jax.ShapeDtypeStruct((128, 1), F32),
        ),
        in_specs=[anywhere] * 4 + [smem] * 2 + [anywhere] * 5,
        out_specs=(vmem, vmem),
        scratch_shapes=[
            pltpu.VMEM((2, LEN, 1280), BF16),
            pltpu.VMEM((2, QUARTER, 5120), BF16),
            pltpu.VMEM((LEN, 1280), BF16),
            pltpu.VMEM((QUARTER, 5120), BF16),
            pltpu.VMEM((R, 1280), BF16),
            pltpu.VMEM((R, 5120), BF16),
            pltpu.VMEM((R, R), F32),
            pltpu.VMEM((R, R), F32),
            pltpu.VMEM((512, 4096), BF16),
            pltpu.VMEM((4, R, 2 * QUARTER), BF16),
            pltpu.VMEM((4, 2, 8, 128), F32),
            pltpu.VMEM((3, 2, 8, 128), F32),
            pltpu.VMEM((16, 128), BF16),
            pltpu.VMEM((4, 8, 16, 128), BF16),
            pltpu.VMEM((8, 128), F32),
            pltpu.VMEM((2, CHUNKS, 4, 32, CHUNK), BF16),
            pltpu.VMEM((2, 128, 512), F32),
            pltpu.VMEM((2, 128, 16), F32),
            pltpu.VMEM((4, R, QUARTER), BF16),
            pltpu.VMEM((R, R), F32),
            pltpu.VMEM((32, 128), F32),
            pltpu.VMEM((3, 32, 128), F32),
            pltpu.VMEM((16, 4096), F32),
            pltpu.VMEM((16, 4096), BF16),
            dma((9,)),
            dma((3,)),
            dma((3,)),
            dma((3,)),
            dma((3,)),
            dma((8,)),
            dma((8,)),
            dma((3,)),
            dma((3,)),
            dma((CHUNKS, 3)),
            dma((CHUNKS, 3)),
            dma((CHUNKS, 4)),
            dma((CHUNKS, 4)),
            dma((3,)),
            dma((3,)),
            dma((3,)),
            dma((3,)),
        ],
        compiler_params=pltpu.CompilerParams(
            collective_id=0, has_side_effects=True, vmem_limit_bytes=48 * 1024 * 1024
        ),
    )(*args)


def solution(mesh):
    return jax.shard_map(
        body,
        mesh=mesh,
        in_specs=(
            P("store", None, "tensor"),
            P("store", "tensor", None),
            P("store", None, "tensor"),
            P("store", "tensor", None),
            P("store"),
            P("store"),
            P(None, "tensor"),
            P(),
            P(),
            P(),
            P(("store", "tensor"), None),
        ),
        out_specs=(P(None, ("store", "tensor")), P(None, "store")),
        check_vma=False,
    )
```

```python
import jax
import jax.numpy as jnp
from jax import lax
from jax.experimental import pallas as pl
from jax.experimental.pallas import tpu as pltpu
from jax.sharding import PartitionSpec as P

MESH = pl.DeviceIdType.MESH
F32 = jnp.float32
BF16 = jnp.bfloat16
HIGHEST = lax.Precision.HIGHEST
NT = (((1,), (1,)), ((), ()))

R = 64
QUARTER = 128
LEN = 512
HALF = 2048


def remote(src, dst, send_sem, recv_sem, device):
    return pltpu.make_async_remote_copy(
        src_ref=src,
        dst_ref=dst,
        send_sem=send_sem,
        recv_sem=recv_sem,
        device_id=device,
        device_id_type=MESH,
    )


def mod4(value):
    return lax.rem(value + 4, 4)


def kernel(
    tin_ref,
    tcot_ref,
    rin_ref,
    rcot_ref,
    tlen_ref,
    rlen,
    win_ref,
    wout_ref,
    iinv_ref,
    oinv_ref,
    store_ref,
    scores_ref,
    fresh_ref,
    tin,
    tcot,
    rin,
    rcot,
    win,
    wout,
    iinv,
    oinv,
    tlen,
    store,
    storep,
    po_send,
    po,
    pi_send,
    pi,
    mine,
    col,
    full,
    lhs,
    acc,
    accf,
    rpo,
    rscr,
    rpart_send,
    rpart_recv,
    trow,
    trowb,
    load_sem,
    po_ss,
    po_rs,
    pi_ss,
    pi_rs,
    col_ss,
    col_rs,
    s4_ss,
    s4_rs,
    s5_ss,
    s5_rs,
    fw_ss,
    fw_rs,
    rpo_ss,
    rpo_rs,
    rrs_ss,
    rrs_rs,
):
    me = lax.axis_index("store")
    t = lax.axis_index("tensor")
    c = lax.rem(me, 2)
    y = lax.rem(lax.div(me, 2), 4)
    zl = lax.rem(lax.div(me, 8), 2)
    x = lax.div(me, 16)

    def index(xx, zz, yy, cc):
        return ((xx * 2 + zz) * 4 + yy) * 2 + cc

    barrier = pltpu.get_barrier_semaphore()
    partners = [(me, mod4(t + 2)), (me, mod4(t + 1)), (me, mod4(t + 3))]
    for dt in (2, 1, 3, 0):
        for dz in range(2):
            for dc in range(2):
                if dz or dc:
                    partners.append(
                        (index(x, lax.rem(zl + dz, 2), y, lax.rem(c + dc, 2)), mod4(t + dt))
                    )
    for k in range(1, 4):
        partners.append((index(mod4(x + k), zl, y, c), t))
        partners.append((index(x, zl, mod4(y + k), c), t))

    load_wout = pltpu.make_async_copy(wout_ref, wout, load_sem.at[0])
    load_cot = [
        pltpu.make_async_copy(tcot_ref.at[n], tcot.at[n], load_sem.at[1 + n]) for n in range(2)
    ]
    load_oinv = pltpu.make_async_copy(oinv_ref, oinv, load_sem.at[3])
    load_iinv = pltpu.make_async_copy(iinv_ref, iinv, load_sem.at[4])
    load_win = pltpu.make_async_copy(win_ref, win, load_sem.at[5])
    load_in = [
        pltpu.make_async_copy(tin_ref.at[n], tin.at[n], load_sem.at[6 + n]) for n in range(2)
    ]
    load_tlen = pltpu.make_async_copy(tlen_ref, tlen, load_sem.at[8])
    load_rcot = pltpu.make_async_copy(rcot_ref.at[0], rcot, load_sem.at[10])
    load_rin = pltpu.make_async_copy(rin_ref.at[0], rin, load_sem.at[11])
    load_store = pltpu.make_async_copy(store_ref, store, load_sem.at[12])
    for partner in partners[:3]:
        pl.semaphore_signal(barrier, inc=1, device_id=partner, device_id_type=MESH)
    for copy in [load_wout, *load_cot, load_oinv, load_tlen, load_win, load_iinv, *load_in]:
        copy.start()
    for partner in partners[3:]:
        pl.semaphore_signal(barrier, inc=1, device_id=partner, device_id_type=MESH)

    lane = lax.broadcasted_iota(jnp.int32, (1, QUARTER), 1) + t * QUARTER

    def scale_of(length):
        lengths = jnp.full((1, QUARTER), length, jnp.int32)
        kept = jnp.where(lane < lengths, 1.0, 0.0).astype(F32)
        return kept / lengths.astype(F32)

    load_wout.wait()
    for copy in load_cot:
        copy.wait()
    pout = lax.dot_general(
        wout[...], tcot[...].reshape(2 * QUARTER, 5120), NT, preferred_element_type=F32
    )
    load_tlen.wait()
    scale = jnp.concatenate([scale_of(tlen[0]), scale_of(tlen[1])], axis=1)
    pout = pout * scale
    load_oinv.wait()
    left = jnp.concatenate([oinv[pl.ds(r, 16, stride=4), :] for r in range(4)], axis=0)
    pout = jnp.dot(left, pout, precision=HIGHEST, preferred_element_type=F32).astype(BF16)
    for n in range(2):
        po_send[n] = pout[:, n * QUARTER : (n + 1) * QUARTER]

    pl.semaphore_wait(barrier, len(partners))
    po_copies = []
    for k in (2, 1, 3):
        to = mod4(t + k)
        copy = remote(
            po_send.at[lax.div(to, 2)], po.at[t], po_ss.at[k - 1], po_rs.at[k - 1], (me, to)
        )
        copy.start()
        po_copies.append(copy)
    po[t] = po_send[lax.div(t, 2)]

    load_iinv.wait()
    load_win.wait()
    for copy in load_in:
        copy.wait()
    pin = lax.dot_general(
        win[...], tin[...].reshape(2 * LEN, 1280), NT, preferred_element_type=F32
    )
    pin = jnp.dot(iinv[...], pin, precision=HIGHEST, preferred_element_type=F32).astype(BF16)
    for u in range(4):
        n, d = u // 2, u % 2
        pi_send[u] = pin[d * 32 : d * 32 + 32, n * LEN : (n + 1) * LEN]
    pi_copies = []
    for k in (2, 1, 3):
        to = mod4(t + k)
        copy = remote(pi_send.at[to], pi.at[k - 1], pi_ss.at[k - 1], pi_rs.at[k - 1], (me, to))
        copy.start()
        pi_copies.append(copy)
    for copy in (load_rcot, load_rin, load_store):
        copy.start()

    load_rcot.wait()
    rout = lax.dot_general(wout[...], rcot[...], NT, preferred_element_type=F32)
    rout = rout * scale_of(rlen[0])
    rpo[t] = rout.astype(BF16)
    load_rin.wait()
    rpin = lax.dot_general(win[...], rin[...], NT, preferred_element_type=F32).astype(BF16)

    for k in (2, 1, 3):
        slot_in = mod4(t - k)
        remote(
            po.at[slot_in], po.at[slot_in], po_ss.at[k - 1], po_rs.at[k - 1], (me, slot_in)
        ).wait_recv()
    outs = jnp.concatenate([po[u] for u in range(4)], axis=1)
    part = lax.dot_general(outs, pi_send[t], NT, preferred_element_type=F32)
    for copy in pi_copies[1:] + pi_copies[:1]:
        copy.wait_recv()
    for k in range(3):
        part += lax.dot_general(outs, pi[k], NT, preferred_element_type=F32)
    mine[...] = jnp.concatenate([part[16 * r : 16 * r + 16] for r in range(4)], axis=1).astype(BF16)

    n = lax.div(t, 2)
    h = lax.rem(t, 2)
    slot = (zl * 2 + c) * 2 + n
    col_copies = []
    for dt, dz in ((2, 0), (2, 1), (1, 1), (3, 1), (1, 0), (3, 0), (0, 1)):
        i = dt * 2 + dz
        copy = remote(
            mine,
            col.at[slot],
            col_ss.at[i],
            col_rs.at[slot],
            (index(x, lax.rem(zl + dz, 2), y, h), mod4(t + dt)),
        )
        copy.start()
        col_copies.append(copy)
    own_copy = pltpu.make_async_copy(mine, col.at[slot], col_rs.at[slot])
    sib_copy = remote(mine, col.at[slot], col_ss.at[0], col_rs.at[slot], (index(x, zl, y, h), t))

    @pl.when(h == c)
    def _():
        own_copy.start()

    @pl.when(h != c)
    def _():
        sib_copy.start()

    rpo_copies = []
    for k in (2, 1, 3):
        copy = remote(
            rpo.at[t], rpo.at[t], rpo_ss.at[k - 1], rpo_rs.at[k - 1], (me, mod4(t + k))
        )
        copy.start()
        rpo_copies.append(copy)

    load_store.wait()
    from_lane = lax.broadcasted_iota(jnp.int32, (256, 256), 0)
    to_lane = lax.broadcasted_iota(jnp.int32, (256, 256), 1)
    target = (
        lax.rem(lax.div(from_lane, 32), 2) * 128
        + lax.div(from_lane, 64) * 32
        + lax.rem(from_lane, 32)
    )
    order = jnp.where(to_lane == target, 1.0, 0.0).astype(BF16)

    @pl.loop(0, 16)
    def _(g):
        moved = jnp.dot(
            store[:, pl.ds(pl.multiple_of(g * 256, 256), 256)], order, preferred_element_type=F32
        ).astype(BF16)
        at = pl.ds(pl.multiple_of(g * 128, 128), 128)
        storep[0, :, at] = moved[:, :128]
        storep[1, :, at] = moved[:, 128:]

    for i in range(8):
        pltpu.make_async_copy(mine, col.at[i], col_rs.at[i]).wait()

    for g in range(2):
        rows = jnp.swapaxes(col[:, 8 * g : 8 * g + 8, :].astype(F32), 0, 1)
        rows = rows.reshape(4, 16, 128).astype(BF16)
        full[c, x, y, 4 * g : 4 * g + 4] = rows

    first = x * (1 - c) + y * c
    second = y * (1 - c) + x * c
    sib = index(x, zl, y, 1 - c)

    def block(core, i, k, one, two):
        one, two = mod4(one - i), mod4(two - k)
        return full.at[core, one * (1 - core) + two * core, two * (1 - core) + one * core]

    s4_copies, s5_copies, fw_copies = [], [], []

    def send_first(k):
        to = index(mod4(x + k * (1 - c)), zl, mod4(y + k * c), c)
        ref = block(c, 0, 0, first, second)
        copy = remote(ref, ref, s4_ss.at[k - 1], s4_rs.at[k - 1], (to, t))
        copy.start()
        s4_copies.append(copy)

    def send_second(i, k):
        to = index(mod4(x + k * c), zl, mod4(y + k * (1 - c)), c)
        ref = block(c, i, 0, first, second)
        copy = remote(ref, ref, s5_ss.at[i, k - 1], s5_rs.at[i, k - 1], (to, t))
        copy.start()
        s5_copies.append(copy)

    def send_sibling(i, k):
        ref = block(c, i, k, first, second)
        copy = remote(ref, ref, fw_ss.at[i, k], fw_rs.at[i, k], (sib, t))
        copy.start()
        fw_copies.append(copy)

    def take(ref, send_sem, recv_sem):
        remote(ref, ref, send_sem, recv_sem, (sib, t)).wait_recv()

    for k in (2, 1, 3):
        send_first(k)
    for k in (2, 1, 3):
        send_second(0, k)
    send_sibling(0, 0)

    for k in (1, 3, 2):
        from_t = mod4(t - k)
        take(rpo.at[from_t], rpo_ss.at[k - 1], rpo_rs.at[k - 1])
    routs = jnp.concatenate([rpo[u] for u in range(4)], axis=1)
    rscr[...] = lax.dot_general(routs, rpin, NT, preferred_element_type=F32)
    for d in range(2):
        rpart_send[d] = jnp.concatenate(
            [rscr[pl.ds(r, 16, stride=4), :][:, 32 * d : 32 * d + 32] for r in range(4)], axis=1
        )
    rrs_copies = []
    for k in (2, 1, 3):
        copy = remote(
            rpart_send,
            rpart_recv.at[k - 1],
            rrs_ss.at[k - 1],
            rrs_rs.at[k - 1],
            (me, mod4(t + k)),
        )
        copy.start()
        rrs_copies.append(copy)

    for i in (1, 3, 2):
        take(block(c, i, 0, first, second), s4_ss.at[i - 1], s4_rs.at[i - 1])
        for k in (2, 1, 3):
            send_second(i, k)
        send_sibling(i, 0)
    for i in (0, 1, 3, 2):
        for k in (1, 3, 2):
            take(block(c, i, k, first, second), s5_ss.at[i, k - 1], s5_rs.at[i, k - 1])
            send_sibling(i, k)

    for copy in rrs_copies:
        copy.wait_recv()
    rtotal = rpart_send[...] + rpart_recv[0] + rpart_recv[1] + rpart_recv[2]
    trow[...] = jnp.zeros_like(trow)
    for d in range(2):
        for e in range(16):
            trow[d, 0:1, e * 128 : (e + 1) * 128] = rtotal[d, e : e + 1]
    trowb[...] = trow[...].astype(BF16)

    def gather_rows(core):
        for g in range(8):
            tiles = full[core, :, :, g].astype(F32).reshape(16, 2, 8, 128)
            for e in range(2):
                at = (2 * g + e) * 128
                lhs[:, at : at + 128] = tiles[:, e].reshape(128, 128).astype(BF16)

    gather_rows(c)
    acc[...] = lax.dot_general(lhs[...], storep[c], NT, preferred_element_type=F32)
    accf[:, 0:16] = lax.dot_general(lhs[...], trowb[c], NT, preferred_element_type=F32)
    for i in (0, 1, 3, 2):
        for k in (0, 1, 3, 2):
            take(block(1 - c, i, k, second, first), fw_ss.at[i, k], fw_rs.at[i, k])
    gather_rows(1 - c)
    acc[...] += lax.dot_general(lhs[...], storep[1 - c], NT, preferred_element_type=F32)
    accf[:, 0:16] += lax.dot_general(lhs[...], trowb[1 - c], NT, preferred_element_type=F32)

    columns = []
    for xx in range(4):
        for zz in range(2):
            for yp in range(2):
                row = xx * 32 + zz * 16 + yp * 8
                at = [(xx * 4 + yy) * 8 + zz * 4 for yy in (2 * yp, 2 * yp + 1)]
                scores_ref[row : row + 8, :] = jnp.concatenate(
                    [acc[i : i + 4, :] for i in at], axis=0
                )
                columns += [accf[i : i + 4, :] for i in at]
    fresh_ref[...] = jnp.swapaxes(jnp.concatenate(columns, axis=0), 0, 1)[0:1]

    for copy in (
        po_copies
        + pi_copies
        + col_copies
        + rpo_copies
        + s4_copies
        + rrs_copies
        + s5_copies
        + fw_copies
    ):
        copy.wait_send()

    @pl.when(h != c)
    def _():
        sib_copy.wait_send()


def body(*args):
    args = [
        arg if arg.shape == (1,) else pltpu.with_memory_space_constraint(arg, pltpu.HBM)
        for arg in args
    ]
    dma = pltpu.SemaphoreType.DMA
    hbm = pl.BlockSpec(memory_space=pltpu.HBM)
    vmem = pl.BlockSpec(memory_space=pltpu.VMEM)
    scores, fresh = pl.pallas_call(
        kernel,
        out_shape=(
            jax.ShapeDtypeStruct((128, 512), F32),
            jax.ShapeDtypeStruct((1, 128), F32),
        ),
        in_specs=[hbm] * 5 + [pl.BlockSpec(memory_space=pltpu.SMEM)] + [hbm] * 5,
        out_specs=(vmem, vmem),
        scratch_shapes=[
            pltpu.VMEM((2, LEN, 1280), BF16),
            pltpu.VMEM((2, QUARTER, 5120), BF16),
            pltpu.VMEM((LEN, 1280), BF16),
            pltpu.VMEM((QUARTER, 5120), BF16),
            pltpu.VMEM((R, 1280), BF16),
            pltpu.VMEM((R, 5120), BF16),
            pltpu.VMEM((R, R), F32),
            pltpu.VMEM((R, R), F32),
            pltpu.SMEM((2,), jnp.int32),
            pltpu.VMEM((512, 4096), BF16),
            pltpu.VMEM((2, 512, HALF), BF16),
            pltpu.VMEM((2, R, QUARTER), BF16),
            pltpu.VMEM((4, R, QUARTER), BF16),
            pltpu.VMEM((4, 32, LEN), BF16),
            pltpu.VMEM((3, 32, LEN), BF16),
            pltpu.VMEM((16, 128), BF16),
            pltpu.VMEM((8, 16, 128), BF16),
            pltpu.VMEM((2, 4, 4, 8, 16, 128), BF16),
            pltpu.VMEM((128, HALF), BF16),
            pltpu.VMEM((128, 512), F32),
            pltpu.VMEM((128, 128), F32),
            pltpu.VMEM((4, R, QUARTER), BF16),
            pltpu.VMEM((R, R), F32),
            pltpu.VMEM((2, 16, 128), F32),
            pltpu.VMEM((3, 2, 16, 128), F32),
            pltpu.VMEM((2, 16, HALF), F32),
            pltpu.VMEM((2, 16, HALF), BF16),
            dma((13,)),
            dma((3,)),
            dma((3,)),
            dma((3,)),
            dma((3,)),
            dma((8,)),
            dma((8,)),
            dma((3,)),
            dma((3,)),
            dma((4, 3)),
            dma((4, 3)),
            dma((4, 4)),
            dma((4, 4)),
            dma((3,)),
            dma((3,)),
            dma((3,)),
            dma((3,)),
        ],
        compiler_params=pltpu.CompilerParams(
            collective_id=0, has_side_effects=True, vmem_limit_bytes=40 * 1024 * 1024
        ),
    )(*args)
    return scores, fresh.reshape(128, 1)


def solution(mesh):
    return jax.shard_map(
        body,
        mesh=mesh,
        in_specs=(
            P("store", None, "tensor"),
            P("store", "tensor", None),
            P("store", None, "tensor"),
            P("store", "tensor", None),
            P("store"),
            P("store"),
            P(None, "tensor"),
            P(),
            P(),
            P(),
            P(("store", "tensor"), None),
        ),
        out_specs=(P(None, ("store", "tensor")), P(None, "store")),
        check_vma=False,
    )
```

```python
import jax
import jax.numpy as jnp
from jax import lax
from jax.experimental import pallas as pl
from jax.experimental.pallas import tpu as pltpu
from jax.sharding import PartitionSpec as P

MESH = pl.DeviceIdType.MESH
F32 = jnp.float32
BF16 = jnp.bfloat16
NT = (((1,), (1,)), ((), ()))

R = 64
QUARTER = 128
LEN = 512
HALF = 2048


def remote(src, dst, send_sem, recv_sem, device):
    return pltpu.make_async_remote_copy(
        src_ref=src,
        dst_ref=dst,
        send_sem=send_sem,
        recv_sem=recv_sem,
        device_id=device,
        device_id_type=MESH,
    )


def split(value):
    high = value.astype(BF16)
    return high, (value - high.astype(F32)).astype(BF16)


def times(matrix, value):
    mh, ml = split(matrix)
    vh, vl = split(value)
    return jnp.dot(
        jnp.concatenate([mh, ml, mh, ml], axis=1),
        jnp.concatenate([vh, vh, vl, vl], axis=0),
        preferred_element_type=F32,
    )


def mod4(value):
    return lax.rem(value + 4, 4)


def kernel(
    tin_ref,
    tcot_ref,
    rin_ref,
    rcot_ref,
    tlen_ref,
    rlen,
    win_ref,
    wout_ref,
    iinv_ref,
    oinv_ref,
    store_ref,
    scores_ref,
    fresh_ref,
    tin,
    tcot,
    rin,
    rcot,
    win,
    wout,
    iinv,
    oinv,
    tlen,
    store,
    storep,
    pouts,
    pins,
    po_send,
    po,
    pi_send,
    pi,
    mine,
    full,
    rows,
    lhs,
    acc,
    accf,
    rpo,
    rscr,
    rpart_send,
    rpart_recv,
    trow,
    trowb,
    ready,
    load_sem,
    po_ss,
    po_rs,
    pi_ss,
    pi_rs,
    a_ss,
    a_rs,
    b_ss,
    b_rs,
    fw_ss,
    fw_rs,
    rpo_ss,
    rpo_rs,
    rrs_ss,
    rrs_rs,
):
    me = lax.axis_index("store")
    t = lax.axis_index("tensor")
    c = lax.rem(me, 2)
    y = lax.rem(lax.div(me, 2), 4)
    zl = lax.rem(lax.div(me, 8), 2)
    x = lax.div(me, 16)

    def index(xx, zz, yy, cc):
        return ((xx * 2 + zz) * 4 + yy) * 2 + cc

    n = lax.div(t, 2)
    h = lax.rem(t, 2)
    same = h == c
    first = x * (1 - c) + y * c
    second = y * (1 - c) + x * c
    sib = index(x, zl, y, 1 - c)

    load_wout = pltpu.make_async_copy(wout_ref, wout, load_sem.at[0])
    load_cot = pltpu.make_async_copy(tcot_ref, tcot, load_sem.at[1])
    load_oinv = pltpu.make_async_copy(oinv_ref, oinv, load_sem.at[4])
    load_iinv = pltpu.make_async_copy(iinv_ref, iinv, load_sem.at[5])
    load_win = pltpu.make_async_copy(win_ref, win, load_sem.at[6])
    load_in = pltpu.make_async_copy(tin_ref, tin, load_sem.at[7])
    load_tlen = pltpu.make_async_copy(tlen_ref, tlen, load_sem.at[8])
    load_rcot = pltpu.make_async_copy(rcot_ref.at[0], rcot, load_sem.at[9])
    load_rin = pltpu.make_async_copy(rin_ref.at[0], rin, load_sem.at[10])
    load_store = pltpu.make_async_copy(store_ref, store, load_sem.at[11])
    for copy in (load_wout, load_cot):
        copy.start()

    barrier = pltpu.get_barrier_semaphore()
    partners = []
    for dt in (2, 1, 3, 0):
        for dz in range(2):
            for dc in range(2):
                if dt or dz or dc:
                    partners.append(
                        (index(x, lax.rem(zl + dz, 2), y, lax.rem(c + dc, 2)), mod4(t + dt))
                    )
    for k in (2, 1, 3):
        partners.append((index(mod4(x + k), zl, y, c), t))
        partners.append((index(x, zl, mod4(y + k), c), t))
    for partner in partners:
        pl.semaphore_signal(barrier, inc=1, device_id=partner, device_id_type=MESH)
    for copy in (load_oinv, load_tlen, load_win, load_iinv, load_in):
        copy.start()

    lane = lax.broadcasted_iota(jnp.int32, (1, QUARTER), 1) + t * QUARTER

    def scale_of(length):
        lengths = jnp.full((1, QUARTER), length, jnp.int32)
        kept = jnp.where(lane < lengths, 1.0, 0.0).astype(F32)
        return kept / lengths.astype(F32)

    for copy in (load_wout, load_cot, load_win, load_in, load_tlen, load_oinv, load_iinv):
        copy.wait()
    pouts[...] = lax.dot_general(
        wout[...], tcot[...].reshape(2 * QUARTER, 5120), NT, preferred_element_type=F32
    )
    pins[...] = lax.dot_general(
        win[...], tin[...].reshape(2 * LEN, 1280), NT, preferred_element_type=F32
    )
    scale = jnp.concatenate([scale_of(tlen[0]), scale_of(tlen[1])], axis=1)
    left = jnp.concatenate([oinv[pl.ds(r, 16, stride=4), :] for r in range(4)], axis=0)
    pout = times(left, pouts[...] * scale).astype(BF16)
    for i in range(2):
        po_send[i] = pout[:, i * QUARTER : (i + 1) * QUARTER]
    pin = times(iinv[...], pins[...]).astype(BF16)
    for u in range(4):
        i, d = u // 2, u % 2
        pi_send[u] = pin[d * 32 : d * 32 + 32, i * LEN : (i + 1) * LEN]

    pl.semaphore_wait(barrier, len(partners))
    po_copies = []
    for k in (2, 1, 3):
        to = mod4(t + k)
        copy = remote(
            po_send.at[lax.div(to, 2)], po.at[t], po_ss.at[k - 1], po_rs.at[k - 1], (me, to)
        )
        copy.start()
        po_copies.append(copy)
    po[t] = po_send[n]

    pi_copies = []
    for k in (2, 1, 3):
        to = mod4(t + k)
        copy = remote(pi_send.at[to], pi.at[k - 1], pi_ss.at[k - 1], pi_rs.at[k - 1], (me, to))
        copy.start()
        pi_copies.append(copy)
    off = lax.rem(h + c, 2)
    for dt in (2, 0):
        for dz in range(2):
            for dc in range(2):
                whom = (
                    index(x, lax.rem(zl + dz, 2), y, lax.rem(c + dc, 2)),
                    mod4(t + off + dt),
                )
                if dt or dz or dc:
                    pl.semaphore_signal(ready, inc=1, device_id=whom, device_id_type=MESH)
                else:

                    @pl.when(jnp.logical_not(same))
                    def _():
                        pl.semaphore_signal(ready, inc=1, device_id=whom, device_id_type=MESH)

    for copy in (load_rcot, load_rin, load_store):
        copy.start()

    load_rcot.wait()
    rout = lax.dot_general(wout[...], rcot[...], NT, preferred_element_type=F32)
    rout = rout * scale_of(rlen[0])
    rpo[t] = rout.astype(BF16)
    load_rin.wait()
    rpin = lax.dot_general(win[...], rin[...], NT, preferred_element_type=F32).astype(BF16)

    for k in (2, 1, 3):
        slot_in = mod4(t - k)
        remote(
            po.at[slot_in], po.at[slot_in], po_ss.at[k - 1], po_rs.at[k - 1], (me, slot_in)
        ).wait_recv()
    outs = jnp.concatenate([po[u] for u in range(4)], axis=1)
    part = lax.dot_general(outs, pi_send[t], NT, preferred_element_type=F32)
    for copy in pi_copies[1:] + pi_copies[:1]:
        copy.wait_recv()
    for k in range(3):
        part += lax.dot_general(outs, pi[k], NT, preferred_element_type=F32)
    mine[...] = jnp.concatenate([part[16 * r : 16 * r + 16] for r in range(4)], axis=1).astype(BF16)

    pl.semaphore_wait(ready, 8 - same.astype(jnp.int32))
    slot = n * 4 + zl * 2 + c
    a_copies = []
    for k in (2, 1, 3, 0):
        for dt, dz in ((2, 0), (2, 1), (1, 1), (3, 1), (1, 0), (3, 0), (0, 1), (0, 0)):
            i = (k * 4 + dt) * 2 + dz
            to = index(mod4(x + k * (1 - h)), lax.rem(zl + dz, 2), mod4(y + k * h), h)
            copy = remote(
                mine, full.at[h, x, y, slot], a_ss.at[i], a_rs.at[k, slot], (to, mod4(t + dt))
            )
            if i:
                copy.start()
                a_copies.append(copy)
            else:
                sib_copy = copy
    own_copy = pltpu.make_async_copy(mine, full.at[h, x, y, slot], a_rs.at[0, slot])

    @pl.when(same)
    def _():
        own_copy.start()

    @pl.when(jnp.logical_not(same))
    def _():
        sib_copy.start()

    rpo_copies = []
    for k in (2, 1, 3):
        copy = remote(
            rpo.at[t], rpo.at[t], rpo_ss.at[k - 1], rpo_rs.at[k - 1], (me, mod4(t + k))
        )
        copy.start()
        rpo_copies.append(copy)

    load_store.wait()
    from_lane = lax.broadcasted_iota(jnp.int32, (256, 256), 1)
    to_lane = lax.broadcasted_iota(jnp.int32, (256, 256), 0)
    target = (
        lax.rem(lax.div(from_lane, 32), 2) * 128
        + lax.div(from_lane, 64) * 32
        + lax.rem(from_lane, 32)
    )
    order = jnp.where(to_lane == target, 1.0, 0.0).astype(BF16)

    @pl.loop(0, 16)
    def _(g):
        moved = lax.dot_general(
            order,
            store[:, pl.ds(pl.multiple_of(g * 256, 256), 256)],
            NT,
            preferred_element_type=F32,
        ).astype(BF16)
        at = pl.ds(pl.multiple_of(g * 128, 128), 128)
        storep[0, at, :] = moved[:128]
        storep[1, at, :] = moved[128:]

    def block(core, i, k, one, two, group):
        one, two = mod4(one - i), mod4(two - k)
        return full.at[
            core, one * (1 - core) + two * core, two * (1 - core) + one * core, pl.ds(group * 4, 4)
        ]

    b_copies, fw_copies = [], []

    def send_second(i, k, group):
        to = index(mod4(x + k * c), zl, mod4(y + k * (1 - c)), c)
        ref = block(c, i, 0, first, second, group)
        copy = remote(ref, ref, b_ss.at[i, group, k - 1], b_rs.at[i, group, k - 1], (to, t))
        copy.start()
        b_copies.append(copy)

    def send_sibling(i, k, group):
        ref = block(c, i, k, first, second, group)
        copy = remote(ref, ref, fw_ss.at[i, group, k], fw_rs.at[i, group, k], (sib, t))
        copy.start()
        fw_copies.append(copy)

    def take(ref, send_sem, recv_sem):
        remote(ref, ref, send_sem, recv_sem, (sib, t)).wait_recv()

    def take_first(i, group):
        for j in range(4):
            one = mod4(first - i)
            piece = full.at[c, one * (1 - c) + second * c, second * (1 - c) + one * c, group * 4 + j]
            pltpu.make_async_copy(mine, piece, a_rs.at[i, group * 4 + j]).wait()
        for k in (2, 1, 3):
            send_second(i, k, group)
        send_sibling(i, 0, group)

    near = lax.div(mod4(t - c), 2)
    groups = (near, 1 - near)
    for i in (0, 1, 3, 2):
        take_first(i, near)

    for i in (0, 1, 3, 2):
        take_first(i, 1 - near)

    for k in (1, 3, 2):
        from_t = mod4(t - k)
        take(rpo.at[from_t], rpo_ss.at[k - 1], rpo_rs.at[k - 1])
    routs = jnp.concatenate([rpo[u] for u in range(4)], axis=1)
    rscr[...] = lax.dot_general(routs, rpin, NT, preferred_element_type=F32)
    for d in range(2):
        rpart_send[d] = jnp.concatenate(
            [rscr[pl.ds(r, 16, stride=4), :][:, 32 * d : 32 * d + 32] for r in range(4)], axis=1
        )
    rrs_copies = []
    for k in (2, 1, 3):
        copy = remote(
            rpart_send,
            rpart_recv.at[k - 1],
            rrs_ss.at[k - 1],
            rrs_rs.at[k - 1],
            (me, mod4(t + k)),
        )
        copy.start()
        rrs_copies.append(copy)

    for group in groups:
        for i in (0, 1, 3, 2):
            for k in (1, 3, 2):
                take(
                    block(c, i, k, first, second, group),
                    b_ss.at[i, group, k - 1],
                    b_rs.at[i, group, k - 1],
                )
                send_sibling(i, k, group)

    for copy in rrs_copies:
        copy.wait_recv()
    rtotal = rpart_send[...] + rpart_recv[0] + rpart_recv[1] + rpart_recv[2]
    trow[...] = jnp.zeros_like(trow)
    for d in range(2):
        for e in range(16):
            trow[d, 0:1, e * 128 : (e + 1) * 128] = rtotal[d, e : e + 1]
    trowb[...] = trow[...].astype(BF16)

    def gather_rows(core):
        for xx in range(4):
            for yy in range(4):
                for q in range(8):
                    row = xx * 32 + (q // 2 % 2) * 16 + yy * 4 + q % 2 * 2 + q // 4
                    rows[row * 16 : row * 16 + 16, :] = full[core, xx, yy, q].astype(F32)
        for e in range(16):
            lhs[:, e * 128 : e * 128 + 128] = rows[pl.ds(e, 128, stride=16), :].astype(BF16)

    gather_rows(c)
    acc[...] = jnp.dot(lhs[...], storep[c], preferred_element_type=F32)
    accf[...] = lax.dot_general(trowb[c], lhs[...], NT, preferred_element_type=F32)
    for group in range(2):
        for i in (0, 1, 3, 2):
            for k in (0, 1, 3, 2):
                take(
                    block(1 - c, i, k, second, first, group),
                    fw_ss.at[i, group, k],
                    fw_rs.at[i, group, k],
                )
    gather_rows(1 - c)
    scores_ref[...] = acc[...] + jnp.dot(lhs[...], storep[1 - c], preferred_element_type=F32)
    total = accf[...] + lax.dot_general(trowb[1 - c], lhs[...], NT, preferred_element_type=F32)
    fresh_ref[...] = total[0:1]

    for copy in po_copies + pi_copies + a_copies + rpo_copies + rrs_copies + b_copies + fw_copies:
        copy.wait_send()

    @pl.when(jnp.logical_not(same))
    def _():
        sib_copy.wait_send()


def body(*args):
    args = [
        arg if arg.shape == (1,) else pltpu.with_memory_space_constraint(arg, pltpu.HBM)
        for arg in args
    ]
    dma = pltpu.SemaphoreType.DMA
    hbm = pl.BlockSpec(memory_space=pltpu.HBM)
    vmem = pl.BlockSpec(memory_space=pltpu.VMEM)
    scores, fresh = pl.pallas_call(
        kernel,
        out_shape=(
            jax.ShapeDtypeStruct((128, 512), F32),
            jax.ShapeDtypeStruct((1, 128), F32),
        ),
        in_specs=[hbm] * 5 + [pl.BlockSpec(memory_space=pltpu.SMEM)] + [hbm] * 5,
        out_specs=(vmem, vmem),
        scratch_shapes=[
            pltpu.VMEM((2, LEN, 1280), BF16),
            pltpu.VMEM((2, QUARTER, 5120), BF16),
            pltpu.VMEM((LEN, 1280), BF16),
            pltpu.VMEM((QUARTER, 5120), BF16),
            pltpu.VMEM((R, 1280), BF16),
            pltpu.VMEM((R, 5120), BF16),
            pltpu.VMEM((R, R), F32),
            pltpu.VMEM((R, R), F32),
            pltpu.SMEM((2,), jnp.int32),
            pltpu.VMEM((512, 4096), BF16),
            pltpu.VMEM((2, HALF, 512), BF16),
            pltpu.VMEM((R, 2 * QUARTER), F32),
            pltpu.VMEM((R, 2 * LEN), F32),
            pltpu.VMEM((2, R, QUARTER), BF16),
            pltpu.VMEM((4, R, QUARTER), BF16),
            pltpu.VMEM((4, 32, LEN), BF16),
            pltpu.VMEM((3, 32, LEN), BF16),
            pltpu.VMEM((16, 128), BF16),
            pltpu.VMEM((2, 4, 4, 8, 16, 128), BF16),
            pltpu.VMEM((128 * 16, 128), F32),
            pltpu.VMEM((128, HALF), BF16),
            pltpu.VMEM((128, 512), F32),
            pltpu.VMEM((16, 128), F32),
            pltpu.VMEM((4, R, QUARTER), BF16),
            pltpu.VMEM((R, R), F32),
            pltpu.VMEM((2, 16, 128), F32),
            pltpu.VMEM((3, 2, 16, 128), F32),
            pltpu.VMEM((2, 16, HALF), F32),
            pltpu.VMEM((2, 16, HALF), BF16),
            pltpu.SemaphoreType.REGULAR,
            dma((12,)),
            dma((3,)),
            dma((3,)),
            dma((3,)),
            dma((3,)),
            dma((32,)),
            dma((4, 8)),
            dma((4, 2, 3)),
            dma((4, 2, 3)),
            dma((4, 2, 4)),
            dma((4, 2, 4)),
            dma((3,)),
            dma((3,)),
            dma((3,)),
            dma((3,)),
        ],
        compiler_params=pltpu.CompilerParams(
            collective_id=0, has_side_effects=True, vmem_limit_bytes=40 * 1024 * 1024
        ),
    )(*args)
    return scores, fresh.reshape(128, 1)


def solution(mesh):
    return jax.shard_map(
        body,
        mesh=mesh,
        in_specs=(
            P("store", None, "tensor"),
            P("store", "tensor", None),
            P("store", None, "tensor"),
            P("store", "tensor", None),
            P("store"),
            P("store"),
            P(None, "tensor"),
            P(),
            P(),
            P(),
            P(("store", "tensor"), None),
        ),
        out_specs=(P(None, ("store", "tensor")), P(None, "store")),
        check_vma=False,
    )
```

```python
import jax
import jax.numpy as jnp
from jax import lax
from jax.experimental import pallas as pl
from jax.experimental.pallas import tpu as pltpu
from jax.sharding import PartitionSpec as P

MESH = pl.DeviceIdType.MESH
F32 = jnp.float32
BF16 = jnp.bfloat16
NT = (((1,), (1,)), ((), ()))

R = 64
QUARTER = 128
LEN = 512
HALF = 2048


def remote(src, dst, send_sem, recv_sem, device):
    return pltpu.make_async_remote_copy(
        src_ref=src,
        dst_ref=dst,
        send_sem=send_sem,
        recv_sem=recv_sem,
        device_id=device,
        device_id_type=MESH,
    )


def split(value):
    high = value.astype(BF16)
    return high, (value - high.astype(F32)).astype(BF16)


def times(matrix, value):
    mh, ml = split(matrix)
    vh, vl = split(value)
    return jnp.dot(
        jnp.concatenate([mh, ml, mh, ml], axis=1),
        jnp.concatenate([vh, vh, vl, vl], axis=0),
        preferred_element_type=F32,
    )


def take(ref, sem):
    pltpu.make_async_copy(ref, ref, sem).wait()


def mod4(value):
    return lax.rem(value + 4, 4)


def kernel(
    tin_ref,
    tcot_ref,
    rin_ref,
    rcot_ref,
    tlen_ref,
    rlen,
    win_ref,
    wout_ref,
    iinv_ref,
    oinv_ref,
    store_ref,
    scores_ref,
    fresh_ref,
    tin,
    tcot,
    rin,
    rcot,
    win,
    wout,
    iinv,
    oinv,
    tlen,
    store,
    storep,
    pouts,
    pins,
    po_send,
    po,
    pi_send,
    pi,
    mine,
    full,
    rows,
    lhs,
    acc,
    accf,
    rpo,
    rscr,
    rpart_send,
    rpart_recv,
    trow,
    trowb,
    ready,
    load_sem,
    po_ss,
    po_rs,
    pi_ss,
    pi_rs,
    a_ss,
    a_rs,
    b_ss,
    b_rs,
    fw_ss,
    fw_rs,
    rpo_ss,
    rpo_rs,
    rrs_ss,
    rrs_rs,
):
    me = lax.axis_index("store")
    t = lax.axis_index("tensor")
    c = lax.rem(me, 2)
    y = lax.rem(lax.div(me, 2), 4)
    zl = lax.rem(lax.div(me, 8), 2)
    x = lax.div(me, 16)

    def index(xx, zz, yy, cc):
        return ((xx * 2 + zz) * 4 + yy) * 2 + cc

    n = lax.div(t, 2)
    h = lax.rem(t, 2)
    same = h == c
    first = x * (1 - c) + y * c
    second = y * (1 - c) + x * c
    sib = index(x, zl, y, 1 - c)

    load_wout = pltpu.make_async_copy(wout_ref, wout, load_sem.at[0])
    load_cot = pltpu.make_async_copy(tcot_ref, tcot, load_sem.at[1])
    load_oinv = pltpu.make_async_copy(oinv_ref, oinv, load_sem.at[4])
    load_iinv = pltpu.make_async_copy(iinv_ref, iinv, load_sem.at[5])
    load_win = pltpu.make_async_copy(win_ref, win, load_sem.at[6])
    load_in = pltpu.make_async_copy(tin_ref, tin, load_sem.at[7])
    load_tlen = pltpu.make_async_copy(tlen_ref, tlen, load_sem.at[8])
    load_rcot = pltpu.make_async_copy(rcot_ref.at[0], rcot, load_sem.at[9])
    load_rin = pltpu.make_async_copy(rin_ref.at[0], rin, load_sem.at[10])
    load_store = pltpu.make_async_copy(store_ref, store, load_sem.at[11])
    for copy in (load_wout, load_cot):
        copy.start()

    barrier = pltpu.get_barrier_semaphore()
    partners = []
    for dt in (2, 1, 3, 0):
        for dz in range(2):
            for dc in range(2):
                if dt or dz or dc:
                    partners.append(
                        (index(x, lax.rem(zl + dz, 2), y, lax.rem(c + dc, 2)), mod4(t + dt))
                    )
    for k in (2, 1, 3):
        partners.append((index(mod4(x + k), zl, y, c), t))
        partners.append((index(x, zl, mod4(y + k), c), t))
    for copy in (load_oinv, load_tlen, load_win, load_iinv, load_in):
        copy.start()
    for partner in partners:
        pl.semaphore_signal(barrier, inc=1, device_id=partner, device_id_type=MESH)

    lane = lax.broadcasted_iota(jnp.int32, (1, QUARTER), 1) + t * QUARTER

    def scale_of(length):
        lengths = jnp.full((1, QUARTER), length, jnp.int32)
        kept = jnp.where(lane < lengths, 1.0, 0.0).astype(F32)
        return kept / lengths.astype(F32)

    for copy in (load_wout, load_cot, load_win, load_in, load_tlen, load_oinv, load_iinv):
        copy.wait()
    pouts[...] = lax.dot_general(
        wout[...], tcot[...].reshape(2 * QUARTER, 5120), NT, preferred_element_type=F32
    )
    pins[...] = lax.dot_general(
        win[...], tin[...].reshape(2 * LEN, 1280), NT, preferred_element_type=F32
    )
    scale = jnp.concatenate([scale_of(tlen[0]), scale_of(tlen[1])], axis=1)
    left = jnp.concatenate([oinv[pl.ds(r, 16, stride=4), :] for r in range(4)], axis=0)
    pout = times(left, pouts[...] * scale).astype(BF16)
    for i in range(2):
        po_send[i] = pout[:, i * QUARTER : (i + 1) * QUARTER]
    pin = times(iinv[...], pins[...]).astype(BF16)
    for u in range(4):
        i, d = u // 2, u % 2
        pi_send[u] = pin[d * 32 : d * 32 + 32, i * LEN : (i + 1) * LEN]

    pl.semaphore_wait(barrier, len(partners))
    for k in (2, 1, 3):
        to = mod4(t + k)
        copy = remote(
            po_send.at[lax.div(to, 2)], po.at[t], po_ss, po_rs, (me, to)
        )
        copy.start()
    po[t] = po_send[n]

    for k in (2, 1, 3):
        to = mod4(t + k)
        copy = remote(pi_send.at[to], pi.at[k - 1], pi_ss, pi_rs, (me, to))
        copy.start()
    off = lax.rem(h + c, 2)
    for dt in (2, 0):
        for dz in range(2):
            for dc in range(2):
                whom = (
                    index(x, lax.rem(zl + dz, 2), y, lax.rem(c + dc, 2)),
                    mod4(t + off + dt),
                )
                if dt or dz or dc:
                    pl.semaphore_signal(ready, inc=1, device_id=whom, device_id_type=MESH)
                else:

                    @pl.when(jnp.logical_not(same))
                    def _():
                        pl.semaphore_signal(ready, inc=1, device_id=whom, device_id_type=MESH)

    for copy in (load_rcot, load_rin, load_store):
        copy.start()

    load_rcot.wait()
    rout = lax.dot_general(wout[...], rcot[...], NT, preferred_element_type=F32)
    rout = rout * scale_of(rlen[0])
    rpo[t] = rout.astype(BF16)
    load_rin.wait()
    rpin = lax.dot_general(win[...], rin[...], NT, preferred_element_type=F32).astype(BF16)

    take(po.at[0:3], po_rs)
    outs = jnp.concatenate([po[u] for u in range(4)], axis=1)
    part = lax.dot_general(outs, pi_send[t], NT, preferred_element_type=F32)
    take(pi, pi_rs)
    for k in range(3):
        part += lax.dot_general(outs, pi[k], NT, preferred_element_type=F32)
    mine[...] = jnp.concatenate([part[16 * r : 16 * r + 16] for r in range(4)], axis=1).astype(BF16)

    pl.semaphore_wait(ready, 8 - same.astype(jnp.int32))
    slot = n * 4 + zl * 2 + c
    for k in (2, 1, 3, 0):
        for dt, dz in ((2, 0), (2, 1), (1, 1), (3, 1), (1, 0), (3, 0), (0, 1), (0, 0)):
            i = (k * 4 + dt) * 2 + dz
            to = index(mod4(x + k * (1 - h)), lax.rem(zl + dz, 2), mod4(y + k * h), h)
            copy = remote(
                mine, full.at[h, x, y, slot], a_ss.at[k if i else 4], a_rs.at[k, n], (to, mod4(t + dt))
            )
            if i:
                copy.start()
            else:
                sib_copy = copy
    own_copy = pltpu.make_async_copy(mine, full.at[h, x, y, slot], a_rs.at[0, n])

    @pl.when(same)
    def _():
        own_copy.start()

    @pl.when(jnp.logical_not(same))
    def _():
        sib_copy.start()

    for k in (2, 1, 3):
        remote(rpo.at[t], rpo.at[t], rpo_ss, rpo_rs, (me, mod4(t + k))).start()

    load_store.wait()
    from_lane = lax.broadcasted_iota(jnp.int32, (256, 256), 1)
    to_lane = lax.broadcasted_iota(jnp.int32, (256, 256), 0)
    target = (
        lax.rem(lax.div(from_lane, 32), 2) * 128
        + lax.div(from_lane, 64) * 32
        + lax.rem(from_lane, 32)
    )
    order = jnp.where(to_lane == target, 1.0, 0.0).astype(BF16)

    @pl.loop(0, 16)
    def _(g):
        moved = lax.dot_general(
            order,
            store[:, pl.ds(pl.multiple_of(g * 256, 256), 256)],
            NT,
            preferred_element_type=F32,
        ).astype(BF16)
        at = pl.ds(pl.multiple_of(g * 128, 128), 128)
        storep[0, at, :] = moved[:128]
        storep[1, at, :] = moved[128:]

    def block(core, i, k, one, two, group):
        one, two = mod4(one - i), mod4(two - k)
        return full.at[
            core, one * (1 - core) + two * core, two * (1 - core) + one * core, pl.ds(group * 4, 4)
        ]

    def send_second(i, k, group):
        to = index(mod4(x + k * c), zl, mod4(y + k * (1 - c)), c)
        ref = block(c, i, 0, first, second, group)
        remote(ref, ref, b_ss, b_rs.at[i, group], (to, t)).start()

    def send_sibling(i, k, group):
        ref = block(c, i, k, first, second, group)
        remote(ref, ref, fw_ss, fw_rs, (sib, t)).start()

    def take_first(i, group):
        take(block(c, i, 0, first, second, group), a_rs.at[i, group])
        for k in (2, 1, 3):
            send_second(i, k, group)
        send_sibling(i, 0, group)

    near = lax.div(mod4(t - c), 2)
    groups = (near, 1 - near)
    for i in (0, 1, 3, 2):
        take_first(i, near)

    for i in (0, 1, 3, 2):
        take_first(i, 1 - near)

    take(rpo.at[0:3], rpo_rs)
    routs = jnp.concatenate([rpo[u] for u in range(4)], axis=1)
    rscr[...] = lax.dot_general(routs, rpin, NT, preferred_element_type=F32)
    for d in range(2):
        rpart_send[d] = jnp.concatenate(
            [rscr[pl.ds(r, 16, stride=4), :][:, 32 * d : 32 * d + 32] for r in range(4)], axis=1
        )
    for k in (2, 1, 3):
        copy = remote(
            rpart_send,
            rpart_recv.at[k - 1],
            rrs_ss,
            rrs_rs,
            (me, mod4(t + k)),
        )
        copy.start()

    for group in groups:
        for i in (0, 1, 3, 2):
            take(full.at[c, 0, 0:3, 0:4], b_rs.at[i, group])
            for k in (1, 3, 2):
                send_sibling(i, k, group)

    take(rpart_recv, rrs_rs)
    rtotal = rpart_send[...] + rpart_recv[0] + rpart_recv[1] + rpart_recv[2]
    trow[...] = jnp.zeros_like(trow)
    for d in range(2):
        for e in range(16):
            trow[d, 0:1, e * 128 : (e + 1) * 128] = rtotal[d, e : e + 1]
    trowb[...] = trow[...].astype(BF16)

    def gather_rows(core):
        for xx in range(4):
            for yy in range(4):
                for q in range(8):
                    row = xx * 32 + (q // 2 % 2) * 16 + yy * 4 + q % 2 * 2 + q // 4
                    rows[row * 16 : row * 16 + 16, :] = full[core, xx, yy, q].astype(F32)
        for e in range(16):
            lhs[:, e * 128 : e * 128 + 128] = rows[pl.ds(e, 128, stride=16), :].astype(BF16)

    gather_rows(c)
    acc[...] = jnp.dot(lhs[...], storep[c], preferred_element_type=F32)
    accf[...] = lax.dot_general(trowb[c], lhs[...], NT, preferred_element_type=F32)
    take(full.at[1 - c], fw_rs)
    gather_rows(1 - c)
    scores_ref[...] = acc[...] + jnp.dot(lhs[...], storep[1 - c], preferred_element_type=F32)
    total = accf[...] + lax.dot_general(trowb[1 - c], lhs[...], NT, preferred_element_type=F32)
    fresh_ref[...] = total[0:1]

    take(po.at[0:3], po_ss)
    take(pi, pi_ss)
    for k in range(1, 4):
        take(full.at[0, 0, 0], a_ss.at[k])
    take(full.at[0, 0, 0, 0:7], a_ss.at[0])
    take(rpo.at[0:3], rpo_ss)
    take(rpart_recv, rrs_ss)
    take(full.at[0, 0:3], b_ss)
    take(full.at[0], fw_ss)

    @pl.when(jnp.logical_not(same))
    def _():
        sib_copy.wait_send()


def body(*args):
    args = [
        arg if arg.shape == (1,) else pltpu.with_memory_space_constraint(arg, pltpu.HBM)
        for arg in args
    ]
    dma = pltpu.SemaphoreType.DMA
    hbm = pl.BlockSpec(memory_space=pltpu.HBM)
    vmem = pl.BlockSpec(memory_space=pltpu.VMEM)
    scores, fresh = pl.pallas_call(
        kernel,
        out_shape=(
            jax.ShapeDtypeStruct((128, 512), F32),
            jax.ShapeDtypeStruct((1, 128), F32),
        ),
        in_specs=[hbm] * 5 + [pl.BlockSpec(memory_space=pltpu.SMEM)] + [hbm] * 5,
        out_specs=(vmem, vmem),
        scratch_shapes=[
            pltpu.VMEM((2, LEN, 1280), BF16),
            pltpu.VMEM((2, QUARTER, 5120), BF16),
            pltpu.VMEM((LEN, 1280), BF16),
            pltpu.VMEM((QUARTER, 5120), BF16),
            pltpu.VMEM((R, 1280), BF16),
            pltpu.VMEM((R, 5120), BF16),
            pltpu.VMEM((R, R), F32),
            pltpu.VMEM((R, R), F32),
            pltpu.SMEM((2,), jnp.int32),
            pltpu.VMEM((512, 4096), BF16),
            pltpu.VMEM((2, HALF, 512), BF16),
            pltpu.VMEM((R, 2 * QUARTER), F32),
            pltpu.VMEM((R, 2 * LEN), F32),
            pltpu.VMEM((2, R, QUARTER), BF16),
            pltpu.VMEM((4, R, QUARTER), BF16),
            pltpu.VMEM((4, 32, LEN), BF16),
            pltpu.VMEM((3, 32, LEN), BF16),
            pltpu.VMEM((16, 128), BF16),
            pltpu.VMEM((2, 4, 4, 8, 16, 128), BF16),
            pltpu.VMEM((128 * 16, 128), F32),
            pltpu.VMEM((128, HALF), BF16),
            pltpu.VMEM((128, 512), F32),
            pltpu.VMEM((16, 128), F32),
            pltpu.VMEM((4, R, QUARTER), BF16),
            pltpu.VMEM((R, R), F32),
            pltpu.VMEM((2, 16, 128), F32),
            pltpu.VMEM((3, 2, 16, 128), F32),
            pltpu.VMEM((2, 16, HALF), F32),
            pltpu.VMEM((2, 16, HALF), BF16),
            pltpu.SemaphoreType.REGULAR,
            dma((12,)),
            dma,
            dma,
            dma,
            dma,
            dma((5,)),
            dma((4, 2)),
            dma,
            dma((4, 2)),
            dma,
            dma,
            dma,
            dma,
            dma,
            dma,
        ],
        compiler_params=pltpu.CompilerParams(
            collective_id=0, has_side_effects=True, vmem_limit_bytes=40 * 1024 * 1024
        ),
    )(*args)
    return scores, fresh.reshape(128, 1)


def solution(mesh):
    return jax.shard_map(
        body,
        mesh=mesh,
        in_specs=(
            P("store", None, "tensor"),
            P("store", "tensor", None),
            P("store", None, "tensor"),
            P("store", "tensor", None),
            P("store"),
            P("store"),
            P(None, "tensor"),
            P(),
            P(),
            P(),
            P(("store", "tensor"), None),
        ),
        out_specs=(P(None, ("store", "tensor")), P(None, "store")),
        check_vma=False,
    )
```

```python
import jax
import jax.numpy as jnp
from jax import lax
from jax.experimental import pallas as pl
from jax.experimental.pallas import tpu as pltpu
from jax.sharding import PartitionSpec as P

MESH = pl.DeviceIdType.MESH
F32 = jnp.float32
BF16 = jnp.bfloat16
NT = (((1,), (1,)), ((), ()))

R = 64
QUARTER = 128
LEN = 512
HALF = 2048


def remote(src, dst, send_sem, recv_sem, device):
    return pltpu.make_async_remote_copy(
        src_ref=src,
        dst_ref=dst,
        send_sem=send_sem,
        recv_sem=recv_sem,
        device_id=device,
        device_id_type=MESH,
    )


def split(value):
    high = value.astype(BF16)
    return high, (value - high.astype(F32)).astype(BF16)


def times(matrix, value):
    mh, ml = split(matrix)
    vh, vl = split(value)
    return jnp.dot(
        jnp.concatenate([mh, ml, mh, ml], axis=1),
        jnp.concatenate([vh, vh, vl, vl], axis=0),
        preferred_element_type=F32,
    )


def take(ref, sem):
    pltpu.make_async_copy(ref, ref, sem).wait()


def mod4(value):
    return lax.rem(value + 4, 4)


def kernel(
    tin_ref,
    tcot_ref,
    rin_ref,
    rcot_ref,
    tlen_ref,
    rlen,
    win_ref,
    wout_ref,
    iinv_ref,
    oinv_ref,
    store_ref,
    scores_ref,
    fresh_ref,
    tin,
    tcot,
    rin,
    rcot,
    win,
    wout,
    iinv,
    oinv,
    tlen,
    store,
    storep,
    pouts,
    pins,
    po_send,
    po,
    pi_send,
    pi,
    mine,
    full,
    rows,
    lhs,
    acc,
    accf,
    rpo,
    rscr,
    rpart_send,
    rpart_recv,
    trow,
    trowb,
    ready,
    load_sem,
    po_ss,
    po_rs,
    pi_ss,
    pi_rs,
    a_ss,
    a_rs,
    b_ss,
    b_rs,
    fw_ss,
    fw_rs,
    rpo_ss,
    rpo_rs,
    rrs_ss,
    rrs_rs,
):
    me = lax.axis_index("store")
    t = lax.axis_index("tensor")
    c = lax.rem(me, 2)
    y = lax.rem(lax.div(me, 2), 4)
    zl = lax.rem(lax.div(me, 8), 2)
    x = lax.div(me, 16)

    def index(xx, zz, yy, cc):
        return ((xx * 2 + zz) * 4 + yy) * 2 + cc

    n = lax.div(t, 2)
    h = lax.rem(t, 2)
    same = h == c
    first = x * (1 - c) + y * c
    second = y * (1 - c) + x * c
    sib = index(x, zl, y, 1 - c)

    load_wout = pltpu.make_async_copy(wout_ref, wout, load_sem.at[0])
    load_cot = [
        pltpu.make_async_copy(tcot_ref.at[i], tcot.at[i], load_sem.at[1 + i]) for i in range(2)
    ]
    load_oinv = pltpu.make_async_copy(oinv_ref, oinv, load_sem.at[4])
    load_iinv = pltpu.make_async_copy(iinv_ref, iinv, load_sem.at[5])
    load_win = pltpu.make_async_copy(win_ref, win, load_sem.at[6])
    load_in = [
        pltpu.make_async_copy(tin_ref.at[i], tin.at[i], load_sem.at[pos])
        for i, pos in enumerate((3, 7))
    ]
    load_tlen = pltpu.make_async_copy(tlen_ref, tlen, load_sem.at[8])
    load_rcot = pltpu.make_async_copy(rcot_ref.at[0], rcot, load_sem.at[9])
    load_rin = pltpu.make_async_copy(rin_ref.at[0], rin, load_sem.at[10])
    load_store = pltpu.make_async_copy(store_ref, store, load_sem.at[11])
    for copy in (load_wout, *load_cot):
        copy.start()

    barrier = pltpu.get_barrier_semaphore()
    partners = []
    for dt in (2, 1, 3, 0):
        for dz in range(2):
            for dc in range(2):
                if dt or dz or dc:
                    partners.append(
                        (index(x, lax.rem(zl + dz, 2), y, lax.rem(c + dc, 2)), mod4(t + dt))
                    )
    for k in (2, 1, 3):
        partners.append((index(mod4(x + k), zl, y, c), t))
        partners.append((index(x, zl, mod4(y + k), c), t))
    for copy in (load_oinv, load_tlen, load_win, load_iinv, *load_in):
        copy.start()
    for partner in partners:
        pl.semaphore_signal(barrier, inc=1, device_id=partner, device_id_type=MESH)

    lane = lax.broadcasted_iota(jnp.int32, (1, QUARTER), 1) + t * QUARTER

    def scale_of(length):
        lengths = jnp.full((1, QUARTER), length, jnp.int32)
        kept = jnp.where(lane < lengths, 1.0, 0.0).astype(F32)
        return kept / lengths.astype(F32)

    for copy in (load_wout, *load_cot, load_win, *load_in, load_tlen, load_oinv, load_iinv):
        copy.wait()
    pouts[...] = lax.dot_general(
        wout[...], tcot[...].reshape(2 * QUARTER, 5120), NT, preferred_element_type=F32
    )
    pins[...] = lax.dot_general(
        win[...], tin[...].reshape(2 * LEN, 1280), NT, preferred_element_type=F32
    )
    scale = jnp.concatenate([scale_of(tlen[0]), scale_of(tlen[1])], axis=1)
    left = jnp.concatenate([oinv[pl.ds(r, 16, stride=4), :] for r in range(4)], axis=0)
    pout = times(left, pouts[...] * scale).astype(BF16)
    for i in range(2):
        po_send[i] = pout[:, i * QUARTER : (i + 1) * QUARTER]
    pl.semaphore_wait(barrier, len(partners))
    for k in (2, 1, 3):
        to = mod4(t + k)
        copy = remote(
            po_send.at[lax.div(to, 2)], po.at[t], po_ss, po_rs, (me, to)
        )
        copy.start()
    po[t] = po_send[n]

    pin = times(iinv[...], pins[...]).astype(BF16)
    for u in range(4):
        i, d = u // 2, u % 2
        pi_send[u] = pin[d * 32 : d * 32 + 32, i * LEN : (i + 1) * LEN]

    for k in (2, 1, 3):
        to = mod4(t + k)
        copy = remote(pi_send.at[to], pi.at[k - 1], pi_ss, pi_rs, (me, to))
        copy.start()
    off = lax.rem(h + c, 2)
    for dt in (2, 0):
        for dz in range(2):
            for dc in range(2):
                whom = (
                    index(x, lax.rem(zl + dz, 2), y, lax.rem(c + dc, 2)),
                    mod4(t + off + dt),
                )
                if dt or dz or dc:
                    pl.semaphore_signal(ready, inc=1, device_id=whom, device_id_type=MESH)
                else:

                    @pl.when(jnp.logical_not(same))
                    def _():
                        pl.semaphore_signal(ready, inc=1, device_id=whom, device_id_type=MESH)

    for copy in (load_rcot, load_rin, load_store):
        copy.start()

    load_rcot.wait()
    rout = lax.dot_general(wout[...], rcot[...], NT, preferred_element_type=F32)
    rout = rout * scale_of(rlen[0])
    rpo[t] = rout.astype(BF16)
    load_rin.wait()
    rpin = lax.dot_general(win[...], rin[...], NT, preferred_element_type=F32).astype(BF16)

    take(po.at[0:3], po_rs)
    outs = jnp.concatenate([po[u] for u in range(4)], axis=1)
    part = lax.dot_general(outs, pi_send[t], NT, preferred_element_type=F32)
    take(pi, pi_rs)
    for k in range(3):
        part += lax.dot_general(outs, pi[k], NT, preferred_element_type=F32)
    mine[...] = jnp.concatenate([part[16 * r : 16 * r + 16] for r in range(4)], axis=1).astype(BF16)

    pl.semaphore_wait(ready, 8 - same.astype(jnp.int32))
    slot = n * 4 + zl * 2 + c
    for k in (2, 1, 3, 0):
        for dt, dz in ((2, 0), (2, 1), (1, 1), (3, 1), (1, 0), (3, 0), (0, 1), (0, 0)):
            i = (k * 4 + dt) * 2 + dz
            to = index(mod4(x + k * (1 - h)), lax.rem(zl + dz, 2), mod4(y + k * h), h)
            copy = remote(
                mine, full.at[h, x, y, slot], a_ss.at[k if i else 4], a_rs.at[k, n], (to, mod4(t + dt))
            )
            if i:
                copy.start()
            else:
                sib_copy = copy
    own_copy = pltpu.make_async_copy(mine, full.at[h, x, y, slot], a_rs.at[0, n])

    @pl.when(same)
    def _():
        own_copy.start()

    @pl.when(jnp.logical_not(same))
    def _():
        sib_copy.start()

    for k in (2, 1, 3):
        remote(rpo.at[t], rpo.at[t], rpo_ss, rpo_rs, (me, mod4(t + k))).start()

    load_store.wait()
    from_lane = lax.broadcasted_iota(jnp.int32, (256, 256), 1)
    to_lane = lax.broadcasted_iota(jnp.int32, (256, 256), 0)
    target = (
        lax.rem(lax.div(from_lane, 32), 2) * 128
        + lax.div(from_lane, 64) * 32
        + lax.rem(from_lane, 32)
    )
    order = jnp.where(to_lane == target, 1.0, 0.0).astype(BF16)

    @pl.loop(0, 16)
    def _(g):
        moved = lax.dot_general(
            order,
            store[:, pl.ds(pl.multiple_of(g * 256, 256), 256)],
            NT,
            preferred_element_type=F32,
        ).astype(BF16)
        at = pl.ds(pl.multiple_of(g * 128, 128), 128)
        storep[0, at, :] = moved[:128]
        storep[1, at, :] = moved[128:]

    def block(core, i, k, one, two, group):
        one, two = mod4(one - i), mod4(two - k)
        return full.at[
            core, one * (1 - core) + two * core, two * (1 - core) + one * core, pl.ds(group * 4, 4)
        ]

    def send_second(i, k, group):
        to = index(mod4(x + k * c), zl, mod4(y + k * (1 - c)), c)
        ref = block(c, i, 0, first, second, group)
        remote(ref, ref, b_ss, b_rs.at[i, group], (to, t)).start()

    def send_sibling(i, k, group):
        ref = block(c, i, k, first, second, group)
        remote(ref, ref, fw_ss, fw_rs, (sib, t)).start()

    def take_first(i, group):
        take(block(c, i, 0, first, second, group), a_rs.at[i, group])
        for k in (2, 1, 3):
            send_second(i, k, group)
        send_sibling(i, 0, group)

    near = lax.div(mod4(t - c), 2)
    groups = (near, 1 - near)
    for i in (0, 1, 3, 2):
        take_first(i, near)

    for i in (0, 1, 3, 2):
        take_first(i, 1 - near)

    take(rpo.at[0:3], rpo_rs)
    routs = jnp.concatenate([rpo[u] for u in range(4)], axis=1)
    rscr[...] = lax.dot_general(routs, rpin, NT, preferred_element_type=F32)
    for d in range(2):
        rpart_send[d] = jnp.concatenate(
            [rscr[pl.ds(r, 16, stride=4), :][:, 32 * d : 32 * d + 32] for r in range(4)], axis=1
        )
    for k in (2, 1, 3):
        copy = remote(
            rpart_send,
            rpart_recv.at[k - 1],
            rrs_ss,
            rrs_rs,
            (me, mod4(t + k)),
        )
        copy.start()

    for group in groups:
        for i in (0, 1, 3, 2):
            take(full.at[c, 0, 0:3, 0:4], b_rs.at[i, group])
            for k in (1, 3, 2):
                send_sibling(i, k, group)

    take(rpart_recv, rrs_rs)
    rtotal = rpart_send[...] + rpart_recv[0] + rpart_recv[1] + rpart_recv[2]
    trow[...] = jnp.zeros_like(trow)
    for d in range(2):
        for e in range(16):
            trow[d, 0:1, e * 128 : (e + 1) * 128] = rtotal[d, e : e + 1]
    trowb[...] = trow[...].astype(BF16)

    def gather_rows(core):
        for xx in range(4):
            for yy in range(4):
                for q in range(8):
                    row = xx * 32 + (q // 2 % 2) * 16 + yy * 4 + q % 2 * 2 + q // 4
                    rows[row * 16 : row * 16 + 16, :] = full[core, xx, yy, q].astype(F32)
        for e in range(16):
            lhs[:, e * 128 : e * 128 + 128] = rows[pl.ds(e, 128, stride=16), :].astype(BF16)

    gather_rows(c)
    acc[...] = jnp.dot(lhs[...], storep[c], preferred_element_type=F32)
    accf[...] = lax.dot_general(trowb[c], lhs[...], NT, preferred_element_type=F32)
    take(full.at[1 - c], fw_rs)
    gather_rows(1 - c)
    scores_ref[...] = acc[...] + jnp.dot(lhs[...], storep[1 - c], preferred_element_type=F32)
    total = accf[...] + lax.dot_general(trowb[1 - c], lhs[...], NT, preferred_element_type=F32)
    fresh_ref[...] = total[0:1]

    take(po.at[0:3], po_ss)
    take(pi, pi_ss)
    for k in range(1, 4):
        take(full.at[0, 0, 0], a_ss.at[k])
    take(full.at[0, 0, 0, 0:7], a_ss.at[0])
    take(rpo.at[0:3], rpo_ss)
    take(rpart_recv, rrs_ss)
    take(full.at[0, 0:3], b_ss)
    take(full.at[0], fw_ss)

    @pl.when(jnp.logical_not(same))
    def _():
        sib_copy.wait_send()


def body(*args):
    args = [
        arg if arg.shape == (1,) else pltpu.with_memory_space_constraint(arg, pltpu.HBM)
        for arg in args
    ]
    dma = pltpu.SemaphoreType.DMA
    hbm = pl.BlockSpec(memory_space=pltpu.HBM)
    vmem = pl.BlockSpec(memory_space=pltpu.VMEM)
    scores, fresh = pl.pallas_call(
        kernel,
        out_shape=(
            jax.ShapeDtypeStruct((128, 512), F32),
            jax.ShapeDtypeStruct((1, 128), F32),
        ),
        in_specs=[hbm] * 5 + [pl.BlockSpec(memory_space=pltpu.SMEM)] + [hbm] * 5,
        out_specs=(vmem, vmem),
        scratch_shapes=[
            pltpu.VMEM((2, LEN, 1280), BF16),
            pltpu.VMEM((2, QUARTER, 5120), BF16),
            pltpu.VMEM((LEN, 1280), BF16),
            pltpu.VMEM((QUARTER, 5120), BF16),
            pltpu.VMEM((R, 1280), BF16),
            pltpu.VMEM((R, 5120), BF16),
            pltpu.VMEM((R, R), F32),
            pltpu.VMEM((R, R), F32),
            pltpu.SMEM((2,), jnp.int32),
            pltpu.VMEM((512, 4096), BF16),
            pltpu.VMEM((2, HALF, 512), BF16),
            pltpu.VMEM((R, 2 * QUARTER), F32),
            pltpu.VMEM((R, 2 * LEN), F32),
            pltpu.VMEM((2, R, QUARTER), BF16),
            pltpu.VMEM((4, R, QUARTER), BF16),
            pltpu.VMEM((4, 32, LEN), BF16),
            pltpu.VMEM((3, 32, LEN), BF16),
            pltpu.VMEM((16, 128), BF16),
            pltpu.VMEM((2, 4, 4, 8, 16, 128), BF16),
            pltpu.VMEM((128 * 16, 128), F32),
            pltpu.VMEM((128, HALF), BF16),
            pltpu.VMEM((128, 512), F32),
            pltpu.VMEM((16, 128), F32),
            pltpu.VMEM((4, R, QUARTER), BF16),
            pltpu.VMEM((R, R), F32),
            pltpu.VMEM((2, 16, 128), F32),
            pltpu.VMEM((3, 2, 16, 128), F32),
            pltpu.VMEM((2, 16, HALF), F32),
            pltpu.VMEM((2, 16, HALF), BF16),
            pltpu.SemaphoreType.REGULAR,
            dma((12,)),
            dma,
            dma,
            dma,
            dma,
            dma((5,)),
            dma((4, 2)),
            dma,
            dma((4, 2)),
            dma,
            dma,
            dma,
            dma,
            dma,
            dma,
        ],
        compiler_params=pltpu.CompilerParams(
            collective_id=0, has_side_effects=True, vmem_limit_bytes=40 * 1024 * 1024
        ),
    )(*args)
    return scores, fresh.reshape(128, 1)


def solution(mesh):
    return jax.shard_map(
        body,
        mesh=mesh,
        in_specs=(
            P("store", None, "tensor"),
            P("store", "tensor", None),
            P("store", None, "tensor"),
            P("store", "tensor", None),
            P("store"),
            P("store"),
            P(None, "tensor"),
            P(),
            P(),
            P(),
            P(("store", "tensor"), None),
        ),
        out_specs=(P(None, ("store", "tensor")), P(None, "store")),
        check_vma=False,
    )
```

```python
import jax
import jax.numpy as jnp
from jax import lax
from jax.experimental import pallas as pl
from jax.experimental.pallas import tpu as pltpu
from jax.sharding import PartitionSpec as P

MESH = pl.DeviceIdType.MESH
F32 = jnp.float32
BF16 = jnp.bfloat16
NT = (((1,), (1,)), ((), ()))

R = 64
QUARTER = 128
LEN = 512
HALF = 2048


def remote(src, dst, send_sem, recv_sem, device):
    return pltpu.make_async_remote_copy(
        src_ref=src,
        dst_ref=dst,
        send_sem=send_sem,
        recv_sem=recv_sem,
        device_id=device,
        device_id_type=MESH,
    )


def split(value):
    high = value.astype(BF16)
    return high, (value - high.astype(F32)).astype(BF16)


def times(matrix, value):
    mh, ml = split(matrix)
    vh, vl = split(value)
    return jnp.dot(
        jnp.concatenate([mh, ml, mh, ml], axis=1),
        jnp.concatenate([vh, vh, vl, vl], axis=0),
        preferred_element_type=F32,
    )


def take(ref, sem):
    pltpu.make_async_copy(ref, ref, sem).wait()


def mod4(value):
    return lax.rem(value + 4, 4)


def kernel(
    tin_ref,
    tcot_ref,
    rin_ref,
    rcot_ref,
    tlen_ref,
    rlen,
    win_ref,
    wout_ref,
    iinv_ref,
    oinv_ref,
    store_ref,
    scores_ref,
    fresh_ref,
    tin,
    tcot,
    rin,
    rcot,
    win,
    wout,
    iinv,
    oinv,
    tlen,
    store,
    storep,
    pouts,
    pins,
    po_send,
    po,
    pi_send,
    pi,
    mine,
    full,
    rows,
    lhs,
    acc,
    accf,
    rpo,
    rscr,
    rpart_send,
    rpart_recv,
    trow,
    trowb,
    ready,
    load_sem,
    po_ss,
    po_rs,
    pi_ss,
    pi_rs,
    a_ss,
    a_rs,
    b_ss,
    b_rs,
    fw_ss,
    fw_rs,
    rpo_ss,
    rpo_rs,
    rrs_ss,
    rrs_rs,
):
    me = lax.axis_index("store")
    t = lax.axis_index("tensor")
    c = lax.rem(me, 2)
    y = lax.rem(lax.div(me, 2), 4)
    zl = lax.rem(lax.div(me, 8), 2)
    x = lax.div(me, 16)

    def index(xx, zz, yy, cc):
        return ((xx * 2 + zz) * 4 + yy) * 2 + cc

    n = lax.div(t, 2)
    h = lax.rem(t, 2)
    same = h == c
    first = x * (1 - c) + y * c
    second = y * (1 - c) + x * c
    sib = index(x, zl, y, 1 - c)

    load_wout = pltpu.make_async_copy(wout_ref, wout, load_sem.at[0])
    load_cot = [
        pltpu.make_async_copy(tcot_ref.at[i], tcot.at[i], load_sem.at[1 + i]) for i in range(2)
    ]
    load_oinv = pltpu.make_async_copy(oinv_ref, oinv, load_sem.at[4])
    load_iinv = pltpu.make_async_copy(iinv_ref, iinv, load_sem.at[5])
    load_win = pltpu.make_async_copy(win_ref, win, load_sem.at[6])
    load_in = [
        pltpu.make_async_copy(tin_ref.at[i], tin.at[i], load_sem.at[pos])
        for i, pos in enumerate((3, 7))
    ]
    load_tlen = pltpu.make_async_copy(tlen_ref, tlen, load_sem.at[8])
    load_rcot = pltpu.make_async_copy(rcot_ref.at[0], rcot, load_sem.at[9])
    load_rin = pltpu.make_async_copy(rin_ref.at[0], rin, load_sem.at[10])
    load_store = pltpu.make_async_copy(store_ref, store, load_sem.at[11])
    for copy in (load_oinv, load_tlen, load_iinv, load_wout, *load_cot, load_win, *load_in):
        copy.start()

    barrier = pltpu.get_barrier_semaphore()
    partners = []
    for dt in (2, 1, 3, 0):
        for dz in range(2):
            for dc in range(2):
                if dt or dz or dc:
                    partners.append(
                        (index(x, lax.rem(zl + dz, 2), y, lax.rem(c + dc, 2)), mod4(t + dt))
                    )
    for k in (2, 1, 3):
        partners.append((index(mod4(x + k), zl, y, c), t))
        partners.append((index(x, zl, mod4(y + k), c), t))
    for partner in partners:
        pl.semaphore_signal(barrier, inc=1, device_id=partner, device_id_type=MESH)

    lane = lax.broadcasted_iota(jnp.int32, (1, QUARTER), 1) + t * QUARTER

    def scale_of(length):
        lengths = jnp.full((1, QUARTER), length, jnp.int32)
        kept = jnp.where(lane < lengths, 1.0, 0.0).astype(F32)
        return kept / lengths.astype(F32)

    for copy in (load_oinv, load_tlen, load_iinv):
        copy.wait()
    left = jnp.concatenate([oinv[pl.ds(r, 16, stride=4), :] for r in range(4)], axis=0)
    scale = jnp.concatenate([scale_of(tlen[0]), scale_of(tlen[1])], axis=1)
    for copy in (load_wout, *load_cot, load_win, *load_in):
        copy.wait()
    pouts[...] = lax.dot_general(
        wout[...], tcot[...].reshape(2 * QUARTER, 5120), NT, preferred_element_type=F32
    )
    pins[...] = lax.dot_general(
        win[...], tin[...].reshape(2 * LEN, 1280), NT, preferred_element_type=F32
    )
    pout = times(left, pouts[...] * scale).astype(BF16)
    for i in range(2):
        po_send[i] = pout[:, i * QUARTER : (i + 1) * QUARTER]
    pl.semaphore_wait(barrier, len(partners))
    for k in (2, 1, 3):
        to = mod4(t + k)
        copy = remote(
            po_send.at[lax.div(to, 2)], po.at[t], po_ss, po_rs, (me, to)
        )
        copy.start()
    po[t] = po_send[n]

    pin = times(iinv[...], pins[...]).astype(BF16)
    for u in range(4):
        i, d = u // 2, u % 2
        pi_send[u] = pin[d * 32 : d * 32 + 32, i * LEN : (i + 1) * LEN]

    for k in (2, 1, 3):
        to = mod4(t + k)
        copy = remote(pi_send.at[to], pi.at[k - 1], pi_ss, pi_rs, (me, to))
        copy.start()
    off = lax.rem(h + c, 2)
    for dt in (2, 0):
        for dz in range(2):
            for dc in range(2):
                whom = (
                    index(x, lax.rem(zl + dz, 2), y, lax.rem(c + dc, 2)),
                    mod4(t + off + dt),
                )
                if dt or dz or dc:
                    pl.semaphore_signal(ready, inc=1, device_id=whom, device_id_type=MESH)
                else:

                    @pl.when(jnp.logical_not(same))
                    def _():
                        pl.semaphore_signal(ready, inc=1, device_id=whom, device_id_type=MESH)

    for copy in (load_rcot, load_rin, load_store):
        copy.start()

    load_rcot.wait()
    rout = lax.dot_general(wout[...], rcot[...], NT, preferred_element_type=F32)
    rout = rout * scale_of(rlen[0])
    rpo[t] = rout.astype(BF16)
    load_rin.wait()
    rpin = lax.dot_general(win[...], rin[...], NT, preferred_element_type=F32).astype(BF16)

    take(po.at[0:3], po_rs)
    outs = jnp.concatenate([po[u] for u in range(4)], axis=1)
    part = lax.dot_general(outs, pi_send[t], NT, preferred_element_type=F32)
    take(pi, pi_rs)
    for k in range(3):
        part += lax.dot_general(outs, pi[k], NT, preferred_element_type=F32)
    mine[...] = jnp.concatenate([part[16 * r : 16 * r + 16] for r in range(4)], axis=1).astype(BF16)

    pl.semaphore_wait(ready, 8 - same.astype(jnp.int32))
    slot = n * 4 + zl * 2 + c
    for k in (2, 1, 3, 0):
        for dt, dz in ((2, 0), (2, 1), (1, 1), (3, 1), (1, 0), (3, 0), (0, 1), (0, 0)):
            i = (k * 4 + dt) * 2 + dz
            to = index(mod4(x + k * (1 - h)), lax.rem(zl + dz, 2), mod4(y + k * h), h)
            copy = remote(
                mine, full.at[h, x, y, slot], a_ss.at[k if i else 4], a_rs.at[k, n], (to, mod4(t + dt))
            )
            if i:
                copy.start()
            else:
                sib_copy = copy
    own_copy = pltpu.make_async_copy(mine, full.at[h, x, y, slot], a_rs.at[0, n])

    @pl.when(same)
    def _():
        own_copy.start()

    @pl.when(jnp.logical_not(same))
    def _():
        sib_copy.start()

    for k in (2, 1, 3):
        remote(rpo.at[t], rpo.at[t], rpo_ss, rpo_rs, (me, mod4(t + k))).start()

    load_store.wait()
    from_lane = lax.broadcasted_iota(jnp.int32, (256, 256), 1)
    to_lane = lax.broadcasted_iota(jnp.int32, (256, 256), 0)
    target = (
        lax.rem(lax.div(from_lane, 32), 2) * 128
        + lax.div(from_lane, 64) * 32
        + lax.rem(from_lane, 32)
    )
    order = jnp.where(to_lane == target, 1.0, 0.0).astype(BF16)

    @pl.loop(0, 16)
    def _(g):
        moved = lax.dot_general(
            order,
            store[:, pl.ds(pl.multiple_of(g * 256, 256), 256)],
            NT,
            preferred_element_type=F32,
        ).astype(BF16)
        at = pl.ds(pl.multiple_of(g * 128, 128), 128)
        storep[0, at, :] = moved[:128]
        storep[1, at, :] = moved[128:]

    def block(core, i, k, one, two, group):
        one, two = mod4(one - i), mod4(two - k)
        return full.at[
            core, one * (1 - core) + two * core, two * (1 - core) + one * core, pl.ds(group * 4, 4)
        ]

    def send_second(i, k, group):
        to = index(mod4(x + k * c), zl, mod4(y + k * (1 - c)), c)
        ref = block(c, i, 0, first, second, group)
        remote(ref, ref, b_ss, b_rs.at[i, group], (to, t)).start()

    def send_sibling(i, k, group):
        ref = block(c, i, k, first, second, group)
        remote(ref, ref, fw_ss, fw_rs, (sib, t)).start()

    def take_first(i, group):
        take(block(c, i, 0, first, second, group), a_rs.at[i, group])
        for k in (2, 1, 3):
            send_second(i, k, group)
        send_sibling(i, 0, group)

    near = lax.div(mod4(t - c), 2)
    groups = (near, 1 - near)
    for i in (0, 1, 3, 2):
        take_first(i, near)

    for i in (0, 1, 3, 2):
        take_first(i, 1 - near)

    take(rpo.at[0:3], rpo_rs)
    routs = jnp.concatenate([rpo[u] for u in range(4)], axis=1)
    rscr[...] = lax.dot_general(routs, rpin, NT, preferred_element_type=F32)
    for d in range(2):
        rpart_send[d] = jnp.concatenate(
            [rscr[pl.ds(r, 16, stride=4), :][:, 32 * d : 32 * d + 32] for r in range(4)], axis=1
        )
    for k in (2, 1, 3):
        copy = remote(
            rpart_send,
            rpart_recv.at[k - 1],
            rrs_ss,
            rrs_rs,
            (me, mod4(t + k)),
        )
        copy.start()

    for group in groups:
        for i in (0, 1, 3, 2):
            take(full.at[c, 0, 0:3, 0:4], b_rs.at[i, group])
            for k in (1, 3, 2):
                send_sibling(i, k, group)

    take(rpart_recv, rrs_rs)
    rtotal = rpart_send[...] + rpart_recv[0] + rpart_recv[1] + rpart_recv[2]
    trow[...] = jnp.zeros_like(trow)
    for d in range(2):
        for e in range(16):
            trow[d, 0:1, e * 128 : (e + 1) * 128] = rtotal[d, e : e + 1]
    trowb[...] = trow[...].astype(BF16)

    def gather_rows(core):
        for xx in range(4):
            for yy in range(4):
                for q in range(8):
                    row = xx * 32 + (q // 2 % 2) * 16 + yy * 4 + q % 2 * 2 + q // 4
                    rows[row * 16 : row * 16 + 16, :] = full[core, xx, yy, q].astype(F32)
        for e in range(16):
            lhs[:, e * 128 : e * 128 + 128] = rows[pl.ds(e, 128, stride=16), :].astype(BF16)

    gather_rows(c)
    acc[...] = jnp.dot(lhs[...], storep[c], preferred_element_type=F32)
    accf[...] = lax.dot_general(trowb[c], lhs[...], NT, preferred_element_type=F32)
    take(full.at[1 - c], fw_rs)
    gather_rows(1 - c)
    scores_ref[...] = acc[...] + jnp.dot(lhs[...], storep[1 - c], preferred_element_type=F32)
    total = accf[...] + lax.dot_general(trowb[1 - c], lhs[...], NT, preferred_element_type=F32)
    fresh_ref[...] = total[0:1]

    take(po.at[0:3], po_ss)
    take(pi, pi_ss)
    for k in range(1, 4):
        take(full.at[0, 0, 0], a_ss.at[k])
    take(full.at[0, 0, 0, 0:7], a_ss.at[0])
    take(rpo.at[0:3], rpo_ss)
    take(rpart_recv, rrs_ss)
    take(full.at[0, 0:3], b_ss)
    take(full.at[0], fw_ss)

    @pl.when(jnp.logical_not(same))
    def _():
        sib_copy.wait_send()


def body(*args):
    args = [
        arg if arg.shape == (1,) else pltpu.with_memory_space_constraint(arg, pltpu.HBM)
        for arg in args
    ]
    dma = pltpu.SemaphoreType.DMA
    hbm = pl.BlockSpec(memory_space=pltpu.HBM)
    vmem = pl.BlockSpec(memory_space=pltpu.VMEM)
    scores, fresh = pl.pallas_call(
        kernel,
        out_shape=(
            jax.ShapeDtypeStruct((128, 512), F32),
            jax.ShapeDtypeStruct((1, 128), F32),
        ),
        in_specs=[hbm] * 5 + [pl.BlockSpec(memory_space=pltpu.SMEM)] + [hbm] * 5,
        out_specs=(vmem, vmem),
        scratch_shapes=[
            pltpu.VMEM((2, LEN, 1280), BF16),
            pltpu.VMEM((2, QUARTER, 5120), BF16),
            pltpu.VMEM((LEN, 1280), BF16),
            pltpu.VMEM((QUARTER, 5120), BF16),
            pltpu.VMEM((R, 1280), BF16),
            pltpu.VMEM((R, 5120), BF16),
            pltpu.VMEM((R, R), F32),
            pltpu.VMEM((R, R), F32),
            pltpu.SMEM((2,), jnp.int32),
            pltpu.VMEM((512, 4096), BF16),
            pltpu.VMEM((2, HALF, 512), BF16),
            pltpu.VMEM((R, 2 * QUARTER), F32),
            pltpu.VMEM((R, 2 * LEN), F32),
            pltpu.VMEM((2, R, QUARTER), BF16),
            pltpu.VMEM((4, R, QUARTER), BF16),
            pltpu.VMEM((4, 32, LEN), BF16),
            pltpu.VMEM((3, 32, LEN), BF16),
            pltpu.VMEM((16, 128), BF16),
            pltpu.VMEM((2, 4, 4, 8, 16, 128), BF16),
            pltpu.VMEM((128 * 16, 128), F32),
            pltpu.VMEM((128, HALF), BF16),
            pltpu.VMEM((128, 512), F32),
            pltpu.VMEM((16, 128), F32),
            pltpu.VMEM((4, R, QUARTER), BF16),
            pltpu.VMEM((R, R), F32),
            pltpu.VMEM((2, 16, 128), F32),
            pltpu.VMEM((3, 2, 16, 128), F32),
            pltpu.VMEM((2, 16, HALF), F32),
            pltpu.VMEM((2, 16, HALF), BF16),
            pltpu.SemaphoreType.REGULAR,
            dma((12,)),
            dma,
            dma,
            dma,
            dma,
            dma((5,)),
            dma((4, 2)),
            dma,
            dma((4, 2)),
            dma,
            dma,
            dma,
            dma,
            dma,
            dma,
        ],
        compiler_params=pltpu.CompilerParams(
            collective_id=0, has_side_effects=True, vmem_limit_bytes=40 * 1024 * 1024
        ),
    )(*args)
    return scores, fresh.reshape(128, 1)


def solution(mesh):
    return jax.shard_map(
        body,
        mesh=mesh,
        in_specs=(
            P("store", None, "tensor"),
            P("store", "tensor", None),
            P("store", None, "tensor"),
            P("store", "tensor", None),
            P("store"),
            P("store"),
            P(None, "tensor"),
            P(),
            P(),
            P(),
            P(("store", "tensor"), None),
        ),
        out_specs=(P(None, ("store", "tensor")), P(None, "store")),
        check_vma=False,
    )
```
